1024 devices in a mesh: depth: 32 (over y, x_lo, core), rows: 32 (over z, x_hi).
Axes of the slice: x: 4 (x_hi: 2, x_lo: 2; x = x_hi * 2 + x_lo), y: 8, z: 16, core: 2. Of those that a mesh axis runs over, the one named last changes fastest.
Arguments:
- projections: bfloat16 [32, 1024, 4096], P('depth', 'rows'), may hold values from -6 to 6
- owner: int32 [4], replicated, may hold values from 0 to 31, as said below
- row_offset: int32 [4, 128], P(None, 'depth'), may hold values from -14 to 14
- band_start: int32 [4, 1024], P(None, 'rows'), may hold values from -16 to 12
- taps: bfloat16 [4, 128, 4], P(None, 'depth'), may hold values from 0.19921875 to 1
Outputs:
- volume: float32 [128, 1024, 4096], P('depth', 'rows')
The draws below stay inside these ranges and needn't reach their ends.
Inputs may be any that keep to these rules, and one draw needn't show every extreme that they name: `owner`: the 4 entries are distinct slots.
All inputs are finite; a program needn't handle non-finite values.
Results may differ from the reference program's by a relative error of at most 0.0003.
Values may be sent and summed in bfloat16 or wider, within the bound.
No kernel may reach another device: no remote copies, remote signals or barrier semaphores. Data moves between devices by JAX's collectives and lax.ppermute only.
A program may use at most 32 MiB of HBM per device.

```python
import jax
import jax.numpy as jnp
from jax import lax

NC = 4096
ROWS_DEV = 32
VIEWS = 4
KB = 4
NS = 128
NR = 1024
SLOTS = 32


def draw_owner(key, part):
    first_key = jax.random.fold_in(key, 11)
    second_key = jax.random.fold_in(key, 23)
    middle = jax.random.permutation(first_key, SLOTS - 2) + 1
    chosen = jnp.concatenate([jnp.array([0, SLOTS - 1], jnp.int32), middle[:VIEWS - 2].astype(jnp.int32)])
    return jax.random.permutation(second_key, chosen).astype(jnp.int32)


def place_ends(entries, rng, least, high):
    spot = [jax.random.randint(jax.random.fold_in(rng, axis), (), 0, length) for axis, length in enumerate(entries.shape)]
    longest = entries.shape.index(max(entries.shape))
    beside = spot[:longest] + [(spot[longest] + 1) % entries.shape[longest]] + spot[longest + 1:]
    return entries.at[tuple(spot)].set(least).at[tuple(beside)].set(high)


def block_levels(stream_key, shape, shards, smallest, high):
    loudness = 1.0
    for axis_at, shards_of in shards:
        heights = jax.random.uniform(jax.random.fold_in(jax.random.fold_in(stream_key, 6), axis_at), (shards_of,), jnp.float32, smallest / len(shards), high / len(shards))
        loudness = loudness * jnp.repeat(jnp.exp(heights), shape[axis_at] // shards_of).reshape((-1,) + (1,) * (len(shape) - 1 - axis_at))
    return loudness


def scatter_about(rng, shape, spread, bound, cuts=(), held_as=jnp.bfloat16):
    result = spread * jax.random.normal(rng, shape, jnp.float32)
    if cuts:
        result = result * block_levels(rng, shape, cuts, -0.22, 0.18)
    return jnp.clip(result, -bound, bound).astype(held_as)


def setup_inputs(seed: int = 0) -> dict:
    key_list = jax.random.split(jax.random.key(seed), 6)
    projections = scatter_about(key_list[0], (SLOTS, NR, NC), 1.0, 6.0, ((0, 32), (1, 32)))
    owner = draw_owner(jax.random.fold_in(key_list[5], 71), 0)
    row_offset = place_ends(jax.random.randint(key_list[2], (VIEWS, NS), -(ROWS_DEV // 2) + 2, ROWS_DEV // 2 - 1), jax.random.fold_in(key_list[2], 1), -(ROWS_DEV // 2) + 2, (ROWS_DEV // 2 - 1) - 1).astype(jnp.int32)
    band_start = place_ends(jax.random.randint(key_list[3], (VIEWS, NR), -(ROWS_DEV // 2), ROWS_DEV // 2 - KB + 1), jax.random.fold_in(key_list[3], 1), -(ROWS_DEV // 2), (ROWS_DEV // 2 - KB + 1) - 1).astype(jnp.int32)
    taps = jnp.clip(0.19921875 + 0.80078125 * jax.random.uniform(key_list[4], (VIEWS, NS, KB), jnp.float32) ** block_levels(key_list[4], (VIEWS, NS, KB), ((1, 32),), -0.2, 0.2), 0.19921875, 1.0).astype(jnp.bfloat16)
    return dict(projections=projections, owner=owner, row_offset=row_offset, band_start=band_start, taps=taps)


RATE = 0.14
INV_KAPPA2 = 0.25


def conduct(diff):
    return diff / (1.0 + diff * diff * INV_KAPPA2)


def sweep(padded, first_slice, first_row, all_slices, all_rows):
    center = padded[1:-1, 1:-1, :]
    count_s = center.shape[0]
    count_r = center.shape[1]
    slice_ids = first_slice + jnp.arange(count_s, dtype=jnp.int32)
    row_ids = first_row + jnp.arange(count_r, dtype=jnp.int32)
    lower = (slice_ids > 0)[:, None, None]
    upper = (slice_ids < all_slices - 1)[:, None, None]
    left = (row_ids > 0)[None, :, None]
    right = (row_ids < all_rows - 1)[None, :, None]
    total = jnp.where(lower, conduct(padded[:-2, 1:-1, :] - center), 0.0)
    total = total + jnp.where(upper, conduct(padded[2:, 1:-1, :] - center), 0.0)
    total = total + jnp.where(left, conduct(padded[1:-1, :-2, :] - center), 0.0)
    total = total + jnp.where(right, conduct(padded[1:-1, 2:, :] - center), 0.0)
    steps = conduct(center[:, :, 1:] - center[:, :, :-1])
    zero_col = jnp.zeros_like(center[:, :, :1])
    total = total + jnp.concatenate([steps, zero_col], axis=2) - jnp.concatenate([zero_col, steps], axis=2)
    return center + RATE * total


def reference(projections, owner, row_offset, band_start, taps):
    detector = jnp.take(projections, owner, axis=0)
    padded_views = jnp.pad(detector, ((0, 0), (ROWS_DEV, ROWS_DEV), (0, 0)))
    weights = taps.astype(jnp.float32)
    row_ids = jnp.arange(NR, dtype=jnp.int32)
    tap_ids = jnp.arange(KB, dtype=jnp.int32)

    def one_slice(slice_no):
        offsets = lax.dynamic_index_in_dim(row_offset, slice_no, axis=1, keepdims=False)
        slice_w = lax.dynamic_index_in_dim(weights, slice_no, axis=1, keepdims=False)
        total = jnp.zeros((NR, NC), jnp.float32)
        for view in range(VIEWS):
            source = row_ids[:, None] + offsets[view] + band_start[view][:, None] + tap_ids[None, :] + ROWS_DEV
            picked = jnp.take(padded_views[view], source.astype(jnp.int32), axis=0).astype(jnp.float32)
            total = total + jnp.sum(picked * slice_w[view][None, :, None], axis=1)
        return total

    volume0 = lax.map(one_slice, jnp.arange(NS, dtype=jnp.int32))
    volume1 = sweep(jnp.pad(volume0, ((1, 1), (1, 1), (0, 0))), 0, 0, NS, NR)
    return sweep(jnp.pad(volume1, ((1, 1), (1, 1), (0, 0))), 0, 0, NS, NR)
```

```python
import functools

import jax
import jax.numpy as jnp
from jax import lax
from jax.experimental import pallas as pl
from jax.experimental.pallas import tpu as pltpu
from jax.sharding import Mesh, PartitionSpec as P

RATE4 = 0.56
F32 = jnp.float32
BF16 = jnp.bfloat16
I32 = jnp.int32

TILE = 32
HERE = 4
VIEWS = 4
BAND = 4
LANES = 128
NC = 4096
SPAN = 3 * VIEWS * TILE
ROWS = 40
DEEP = HERE + 4
WIDE = 512
STEPS = NC // WIDE
DEPTH = ("y", "xl", "core")


def half_conduct(diff):
    return diff / (diff * diff + 4.0)


def interpolation(ids, prm_ref, bands_ref):
    depth, tile, z, xh = ids[0], ids[1], ids[2], ids[3]
    lane = lax.broadcasted_iota(I32, (1, LANES), 1)
    col = lax.broadcasted_iota(I32, (1, SPAN), 1)
    view_of_col = (col >> 5) & 3
    lane_c = lax.broadcasted_iota(I32, (LANES, SPAN), 0)
    view_c = (lax.broadcasted_iota(I32, (LANES, SPAN), 1) >> 5) & 3

    row = lax.broadcasted_iota(I32, (ROWS, 1), 0)
    row = tile * TILE + jnp.where(row < 36, row, row - ROWS)
    last = 32 * TILE - 1
    row = jnp.where(row < 0, -1 - row, jnp.where(row > last, 2 * last + 1 - row, row))
    row_tile = row >> 5
    first_half = xh == 0
    band_a, band_b, band_t = bands_ref[0:1, :], bands_ref[1:2, :], bands_ref[2:3, :]
    before = jnp.where(first_half, band_t, band_a)
    here = jnp.where(first_half, band_a, band_b)
    after = jnp.where(first_half, band_b, band_t)
    picked = jnp.where(row_tile == tile, here, jnp.where(row_tile < tile, before, after))
    picked = jnp.where((lane & 31) == (row & 31), picked, 0.0).astype(BF16)
    same_view = ((lane_c >> 5) == view_c).astype(F32).astype(BF16)
    bands = jnp.dot(picked, same_view, preferred_element_type=F32)

    slot = col >> 7
    third = jnp.where(first_half, 2 * z - 1, 2 * z + 2)
    source = jnp.where(slot == 2, third, 2 * z + slot)
    col_row = jnp.where((source >= 0) & (source < 32), source * TILE + (col & 31), -100000)
    reach = (col_row - row).astype(F32) - bands

    rest = lane - 4 * VIEWS
    lane_slice = jnp.where(rest < 0, lane & 3, (rest >> 2) & 3)
    rest_c = lane_c - 4 * VIEWS
    lane_view = jnp.where(rest_c < 0, lane_c >> 2, rest_c >> 4)
    last_slice = 32 * HERE - 1
    kinds = [rest < 0] + [(rest >= 0) & (rest < 64) & ((rest & 3) == k) for k in range(BAND)]
    held = []
    for i in range(DEEP):
        at = depth * HERE + (i - 2)
        at = jnp.where(at < 0, -1 - at, jnp.where(at > last_slice, 2 * last_slice + 1 - at, at))
        mine = prm_ref[pl.ds(at >> 2, 1), :]
        held.append(jnp.where(lane_slice == (at & 3), mine, 0.0))
    held = jnp.concatenate(held, axis=0)
    stacked = jnp.concatenate([jnp.where(kind, held, 0.0) for kind in kinds], axis=0)
    spread = ((lane_view == view_c) & (rest_c < 64)).astype(F32).astype(BF16)
    table = jnp.dot(stacked.astype(BF16), spread, preferred_element_type=F32)

    parts = []
    for i in range(DEEP):
        gap = reach - table[i : i + 1, :]
        weight = jnp.zeros((ROWS, SPAN), F32)
        for k in range(BAND):
            at = (k + 1) * DEEP + i
            weight = jnp.where(gap == float(k), table[at : at + 1, :], weight)
        parts.append(weight)
    return jnp.concatenate(parts, axis=0).astype(BF16)


def smooth(src, dst_store, first, count, rows, at):
    centre = src[first - 1, :, pl.ds(at, WIDE)]
    ahead = src[first, :, pl.ds(at, WIDE)]
    below = half_conduct(ahead[:rows] - centre[:rows])
    for i in range(count):
        centre = ahead
        ahead = src[first + i + 1, :, pl.ds(at, WIDE)]
        above = half_conduct(ahead[:rows] - centre[:rows])
        total = above - below
        below = above
        step = half_conduct(pltpu.roll(centre, ROWS - 1, 0) - centre)
        total = total + (step - pltpu.roll(step, 1, 0))[:rows]
        wide = src[first + i, :rows, pl.ds(at - LANES, WIDE + 2 * LANES)]
        step = half_conduct(pltpu.roll(wide, WIDE + 2 * LANES - 1, 1) - wide)
        step = step - pltpu.roll(step, 1, 1)
        total = total + step[:, LANES : LANES + WIDE]
        dst_store(i, centre[:rows] + RATE4 * total)


def kernel(ids, prm_ref, bands_ref, own_ref, other_ref, out_ref, weights, v0, v1):
    k = pl.program_id(0)
    core, xl = ids[5], ids[4]

    def block(n):
        return jnp.where(core == 0, n, STEPS - 1 - n)

    @pl.when(k == 0)
    def _():
        weights[...] = interpolation(ids, prm_ref, bands_ref)

    def project(pack, n):
        j = block(n)
        y0 = (j & 3) * 2
        columns = []
        for i in range(2):
            for x in range(2):
                third = pl.ds(4 + (xl ^ x), 1)
                columns.append(
                    jnp.concatenate(
                        [pack[x, y0 + i], pack[2 + x, y0 + i], pack[third, y0 + i][0]], axis=0
                    )
                )
        rows = jnp.concatenate(columns, axis=1)
        found = jnp.dot(weights[...], rows, preferred_element_type=F32)
        at = pl.multiple_of(LANES + j * WIDE, LANES)
        found = found.reshape(DEEP, ROWS, WIDE)
        v0[:, :, pl.ds(at, WIDE)] = found

        @pl.when(j == 0)
        def _():
            v0[:, :, :LANES] = jnp.broadcast_to(found[:, :, :1], (DEEP, ROWS, LANES))

        @pl.when(j == STEPS - 1)
        def _():
            v0[:, :, LANES + NC :] = jnp.broadcast_to(
                found[:, :, WIDE - 1 :], (DEEP, ROWS, LANES)
            )

    @pl.when(k < STEPS // 2)
    def _():
        project(own_ref, k)

    @pl.when((k >= STEPS // 2) & (k < STEPS))
    def _():
        project(other_ref, k)

    @pl.when((k >= 1) & (k <= STEPS))
    def _():
        j = block(k - 1)
        at = pl.multiple_of(LANES + j * WIDE, LANES)

        def store(i, value):
            v1[i, :, pl.ds(at, WIDE)] = value

            @pl.when(j == 0)
            def _():
                v1[i, :, :LANES] = jnp.broadcast_to(value[:, :1], (ROWS, LANES))

            @pl.when(j == STEPS - 1)
            def _():
                v1[i, :, LANES + NC :] = jnp.broadcast_to(value[:, WIDE - 1 :], (ROWS, LANES))

        smooth(v0, store, 1, HERE + 2, ROWS, at)

    @pl.when(k >= 2)
    def _():
        j = block(k - 2)
        at = pl.multiple_of(LANES + j * WIDE, LANES)

        def store(i, value):
            out_ref[i] = value

        smooth(v1, store, 1, HERE, TILE, at)


def finish(ids, prm, bands, own, other):
    def place(k, ids):
        n = jnp.maximum(k - 2, 0)
        return 0, 0, jnp.where(ids[5] == 0, n, STEPS - 1 - n)

    whole = pl.BlockSpec(memory_space=pltpu.VMEM)
    return pl.pallas_call(
        kernel,
        out_shape=jax.ShapeDtypeStruct((HERE, TILE, NC), F32),
        grid_spec=pltpu.PrefetchScalarGridSpec(
            num_scalar_prefetch=1,
            grid=(STEPS + 2,),
            in_specs=[whole] * 4,
            out_specs=pl.BlockSpec((HERE, TILE, WIDE), place),
            scratch_shapes=[
                pltpu.VMEM((DEEP * ROWS, SPAN), BF16),
                pltpu.VMEM((DEEP, ROWS, NC + 2 * LANES), F32),
                pltpu.VMEM((HERE + 2, ROWS, NC + 2 * LANES), F32),
            ],
        ),
        compiler_params=pltpu.CompilerParams(vmem_limit_bytes=32 * 1024 * 1024),
    )(ids, prm, bands, own, other)


def shards(projections, owner, row_offset, band_start, taps):
    stored = projections[0]
    z, xh, xl, core = (lax.axis_index(a) for a in ("z", "xh", "xl", "core"))
    depth, tile = lax.axis_index(DEPTH), lax.axis_index(("z", "xh"))
    ids = jnp.stack([depth, tile, z, xh, xl, core]).astype(I32)

    numbers = jnp.concatenate([row_offset.astype(BF16).reshape(16), taps.reshape(64)])
    numbers = jnp.pad(numbers[None], ((0, 7), (0, LANES - 80)))
    pieces = stored.reshape(TILE, 2, 8, 2, LANES).transpose(2, 3, 1, 0, 4)
    pieces = pieces.reshape(32, TILE, LANES)
    numbers = jnp.broadcast_to(numbers[None], (32, 8, LANES))
    got = lax.all_to_all(jnp.concatenate([pieces, numbers], axis=1), DEPTH, 0, 0, tiled=True)
    prm = got[:, TILE, :].astype(F32)
    views = jnp.concatenate(
        [lax.dynamic_index_in_dim(got, owner[v], keepdims=False)[:TILE] for v in range(VIEWS)]
    )

    band = jnp.pad(band_start.astype(BF16).reshape(1, LANES), ((0, 7), (0, 0)))
    away = [(2 * i + 1, (2 * i + 2) % 32) for i in range(16)]
    away += [(2 * i, (2 * i - 1) % 32) for i in range(16)]
    third = lax.ppermute(jnp.concatenate([views, band]), ("z", "xh"), away)
    both = jnp.concatenate([views, third[: VIEWS * TILE]])

    along = lax.all_to_all(
        jnp.broadcast_to(both[None], (8,) + both.shape), "y", 0, 0, tiled=True
    )
    far = along[:, VIEWS * TILE :]
    swap = [(0, 1), (1, 0)]
    far_pair = lax.ppermute(far, "xl", swap)
    near = jnp.concatenate([along[:, : VIEWS * TILE].reshape(8 * VIEWS * TILE, LANES), band])
    near = lax.all_to_all(
        jnp.broadcast_to(near[None], (4,) + near.shape), ("xh", "xl"), 0, 0, tiled=True
    )
    bands = jnp.stack(
        [near[0, 8 * VIEWS * TILE], near[2, 8 * VIEWS * TILE], third[VIEWS * TILE]]
    ).astype(F32)
    near = near[:, : 8 * VIEWS * TILE].reshape(4, 8, VIEWS * TILE, LANES)
    own = jnp.concatenate([near, far[None], far_pair[None]])
    other = lax.ppermute(own, "core", swap)
    return finish(ids, prm, bands, own, other)


def solution(mesh):
    parted = Mesh(mesh.devices.reshape(8, 2, 2, 16, 2), DEPTH + ("z", "xh"))
    rows = ("z", "xh")
    placed = (
        P(DEPTH, rows, None),
        P(),
        P(None, DEPTH),
        P(None, rows),
        P(None, DEPTH, None),
    )
    return jax.shard_map(
        shards, mesh=parted, in_specs=placed, out_specs=P(DEPTH, rows, None), check_vma=False
    )
```

```python
import functools

import jax
import jax.numpy as jnp
from jax import lax
from jax.experimental import pallas as pl
from jax.experimental.pallas import tpu as pltpu
from jax.sharding import Mesh, PartitionSpec as P

RATE4 = 0.56
F32 = jnp.float32
BF16 = jnp.bfloat16
I32 = jnp.int32

TILE = 32
HERE = 4
VIEWS = 4
BAND = 4
LANES = 128
NC = 4096
SPAN = 3 * VIEWS * TILE
ROWS = 40
DEEP = HERE + 4
WIDE = 1024
BATCH = 16
DEPTH = ("y", "xl", "core")


def half_conduct(diff):
    return diff / (diff * diff + 4.0)


def interpolation(ids, prm_ref, bands_ref):
    depth, tile, xh = ids[0], ids[1], ids[2]
    lane = lax.broadcasted_iota(I32, (1, LANES), 1)
    col = lax.broadcasted_iota(I32, (1, SPAN), 1)
    view_of_col = (col >> 5) & 3
    lane_c = lax.broadcasted_iota(I32, (LANES, SPAN), 0)
    view_c = (lax.broadcasted_iota(I32, (LANES, SPAN), 1) >> 5) & 3

    row = lax.broadcasted_iota(I32, (ROWS, 1), 0)
    row = tile * TILE + jnp.where(row < 36, row, row - ROWS)
    last = 32 * TILE - 1
    row = jnp.where(row < 0, -1 - row, jnp.where(row > last, 2 * last + 1 - row, row))
    row_tile = row >> 5
    first_half = xh == 0
    here, pair, away = bands_ref[0:1, :], bands_ref[1:2, :], bands_ref[2:3, :]
    before = jnp.where(first_half, away, pair)
    after = jnp.where(first_half, pair, away)
    picked = jnp.where(row_tile == tile, here, jnp.where(row_tile < tile, before, after))
    picked = jnp.where((lane & 31) == (row & 31), picked, 0.0).astype(BF16)
    same_view = ((lane_c >> 5) == view_c).astype(F32).astype(BF16)
    bands = jnp.dot(picked, same_view, preferred_element_type=F32)

    slot = col >> 7
    third = jnp.where(first_half, tile - 1, tile + 1)
    pair = jnp.where(first_half, tile + 1, tile - 1)
    source = jnp.where(slot == 0, tile, jnp.where(slot == 1, pair, third))
    col_row = jnp.where((source >= 0) & (source < 32), source * TILE + (col & 31), -100000)
    reach = (col_row - row).astype(F32) - bands

    rest = lane - 4 * VIEWS
    lane_slice = jnp.where(rest < 0, lane & 3, (rest >> 2) & 3)
    rest_c = lane_c - 4 * VIEWS
    lane_view = jnp.where(rest_c < 0, lane_c >> 2, rest_c >> 4)
    last_slice = 32 * HERE - 1
    kinds = [rest < 0] + [(rest >= 0) & (rest < 64) & ((rest & 3) == k) for k in range(BAND)]
    held = []
    for i in range(DEEP):
        at = depth * HERE + (i - 2)
        at = jnp.where(at < 0, -1 - at, jnp.where(at > last_slice, 2 * last_slice + 1 - at, at))
        mine = prm_ref[pl.ds(at >> 2, 1), :]
        held.append(jnp.where(lane_slice == (at & 3), mine, 0.0))
    held = jnp.concatenate(held, axis=0)
    stacked = jnp.concatenate([jnp.where(kind, held, 0.0) for kind in kinds], axis=0)
    spread = ((lane_view == view_c) & (rest_c < 64)).astype(F32).astype(BF16)
    table = jnp.dot(stacked.astype(BF16), spread, preferred_element_type=F32)

    parts = []
    for i in range(DEEP):
        gap = reach - table[i : i + 1, :]
        weight = jnp.zeros((ROWS, SPAN), F32)
        for k in range(BAND):
            at = (k + 1) * DEEP + i
            weight = jnp.where(gap == float(k), table[at : at + 1, :], weight)
        parts.append(weight)
    return jnp.concatenate(parts, axis=0).astype(BF16)


def sweep(src, flow, count, rows, store):
    lane = lax.broadcasted_iota(I32, (rows, LANES), 1)
    first, last = lane == 0, lane == LANES - 1
    tiles = NC // LANES

    def at(t):
        return slice(t * LANES, (t + 1) * LANES)

    for t in range(tiles):
        flow[:rows, at(t)] = half_conduct(src[1, :rows, at(t)] - src[0, :rows, at(t)])

    def one(i, carry):
        came = 0.0
        for t0 in range(0, tiles, BATCH):
            batch = range(t0, t0 + BATCH)
            tall = [src[i + 1, :, at(t)] for t in batch]
            ahead = [src[i + 2, :rows, at(t)] for t in batch]
            behind = [flow[:rows, at(t)] for t in batch]
            centre = [x[:rows] for x in tall]
            turned = [pltpu.roll(x, LANES - 1, 1) for x in centre]
            if t0 + BATCH < tiles:
                turned.append(pltpu.roll(src[i + 1, :rows, at(t0 + BATCH)], LANES - 1, 1))
            ahead = [half_conduct(x - c) for x, c in zip(ahead, centre)]
            total = [x - y for x, y in zip(ahead, behind)]
            step = [half_conduct(pltpu.roll(x, ROWS - 1, 0) - x) for x in tall]
            step = [(x - pltpu.roll(x, 1, 0))[:rows] for x in step]
            total = [x + y for x, y in zip(total, step)]
            step = []
            for n in range(BATCH):
                if n + 1 < len(turned):
                    right = jnp.where(last, turned[n + 1], turned[n])
                    step.append(half_conduct(right - centre[n]))
                else:
                    step.append(jnp.where(last, 0.0, half_conduct(turned[n] - centre[n])))
            goes = [pltpu.roll(x, 1, 1) for x in step]
            total = [x + y for x, y in zip(total, step)]
            left = [jnp.where(first, x, y) for x, y in zip([came] + goes, goes)]
            came = goes[-1]
            total = [c + RATE4 * (x - y) for c, x, y in zip(centre, total, left)]
            for n, t in enumerate(batch):
                flow[:rows, at(t)] = ahead[n]
            for n, t in enumerate(batch):
                store(i, at(t), total[n])
        return carry

    lax.fori_loop(0, count, one, 0)


def kernel(
    ids, prm_ref, bands_ref, own_ref, own_third_ref, other_ref, other_third_ref, out_ref,
    weights, v0, v1, flow, done, sems,
):
    xl, core = ids[3], ids[4]
    weights[...] = interpolation(ids, prm_ref, bands_ref)

    def project(pieces, thirds, first):
        def part(j, carry):
            columns = []
            for i in range(4):
                for x in range(2):
                    at = pl.multiple_of(((x ^ xl) * 8 + 4 * j + i) * LANES, LANES)
                    columns.append(
                        jnp.concatenate(
                            [
                                pieces[pl.ds(at, LANES)],
                                pieces[pl.ds(16 * LANES + at, LANES)],
                                thirds[pl.ds(at, LANES)],
                            ],
                            axis=0,
                        )
                    )
            rows = jnp.concatenate(columns, axis=1)
            found = jnp.dot(weights[...], rows, preferred_element_type=F32)
            at = pl.multiple_of(first + j * WIDE, LANES)
            v0[:, :, pl.ds(at, WIDE)] = found.reshape(DEEP, ROWS, WIDE)
            return carry

        lax.fori_loop(0, NC // 2 // WIDE, part, 0)

    project(own_ref, own_third_ref, core * (NC // 2))
    project(other_ref, other_third_ref, (1 - core) * (NC // 2))

    def keep(i, at, value):
        v1[i, :, at] = value

    sweep(v0, flow, HERE + 2, ROWS, keep)

    def put(i, at, value):
        done[i, :, at] = value

        if at.stop == NC:
            pltpu.make_async_copy(done.at[i], out_ref.at[i], sems.at[i]).start()

    sweep(v1, flow, HERE, TILE, put)
    for i in range(HERE):
        pltpu.make_async_copy(done.at[i], out_ref.at[i], sems.at[i]).wait()


def finish(ids, prm, bands, *pieces):
    whole = pl.BlockSpec(memory_space=pltpu.VMEM)
    return pl.pallas_call(
        kernel,
        out_shape=jax.ShapeDtypeStruct((HERE, TILE, NC), F32),
        in_specs=[pl.BlockSpec(memory_space=pltpu.SMEM)] + [whole] * 6,
        out_specs=pl.BlockSpec(memory_space=pl.ANY),
        scratch_shapes=[
            pltpu.VMEM((DEEP * ROWS, SPAN), BF16),
            pltpu.VMEM((DEEP, ROWS, NC), F32),
            pltpu.VMEM((HERE + 2, ROWS, NC), F32),
            pltpu.VMEM((ROWS, NC), F32),
            pltpu.VMEM((HERE, TILE, NC), F32),
            pltpu.SemaphoreType.DMA((HERE,)),
        ],
        compiler_params=pltpu.CompilerParams(vmem_limit_bytes=32 * 1024 * 1024),
    )(ids, prm, bands, *pieces)


def pack(stored_ref, offset_ref, taps_ref, out_ref):
    lane = lax.broadcasted_iota(I32, (1, LANES), 1)
    rest = lane - 4 * VIEWS
    line = lax.broadcasted_iota(I32, (HERE, LANES), 0)
    pick = (line == (lane & 3)).astype(F32)
    spread = jnp.dot(offset_ref[...].astype(F32), pick, preferred_element_type=F32)
    mine = (line == (lane >> 2)) & (lane < 4 * VIEWS)
    numbers = jnp.sum(jnp.where(mine, spread, 0.0), axis=0, keepdims=True)
    for v in range(VIEWS):
        spread = jnp.dot(taps_ref[v].astype(F32), pick, preferred_element_type=F32)
        mine = (line == ((rest >> 2) & 3)) & (rest >= 0) & ((rest >> 4) == v)
        numbers += jnp.sum(jnp.where(mine, spread, 0.0), axis=0, keepdims=True)
    numbers = jnp.broadcast_to(numbers, (8, LANES)).astype(BF16)
    for y in range(8):
        for xl in range(2):
            for core in range(2):
                at = ((core * 8 + y) * 2 + xl) * LANES
                piece = stored_ref[:, at : at + LANES]
                out_ref[(y * 2 + xl) * 2 + core] = jnp.concatenate([piece, numbers], axis=0)


def shards(projections, owner, row_offset, band_start, taps):
    xh, xl, core = (lax.axis_index(a) for a in ("xh", "xl", "core"))
    depth, tile = lax.axis_index(DEPTH), lax.axis_index(("z", "xh"))
    ids = jnp.stack([depth, tile, xh, xl, core]).astype(I32)

    whole = pl.BlockSpec(memory_space=pltpu.VMEM)
    pieces = pl.pallas_call(
        pack,
        out_shape=jax.ShapeDtypeStruct((32, TILE + 8, LANES), BF16),
        in_specs=[whole] * 3,
        out_specs=whole,
    )(projections[0], row_offset, taps)
    got = lax.all_to_all(pieces, DEPTH, 0, 0, tiled=True)
    prm = got[:, TILE, :].astype(F32)
    views = jnp.concatenate(
        [lax.dynamic_index_in_dim(got, owner[v], keepdims=False)[:TILE] for v in range(VIEWS)]
    )

    size = VIEWS * TILE
    near = lax.all_to_all(jnp.broadcast_to(views[None], (8, size, LANES)), "y", 0, 0, tiled=True)
    near = near.reshape(8 * size, LANES)

    band = jnp.pad(band_start.astype(BF16).reshape(1, LANES), ((0, 7), (0, 0)))
    swap = [(0, 1), (1, 0)]
    cross = [(0, 3), (1, 2), (2, 1), (3, 0)]
    pair = lax.ppermute(jnp.concatenate([near, band]), "xh", swap)
    pair_far = lax.ppermute(near, ("xl", "xh"), cross)
    near_late, pair_far = lax.optimization_barrier((near, pair_far))
    near_far = lax.ppermute(near_late, "xl", swap)

    along = [(2 * i, (2 * i + 2) % 32) for i in range(16)]
    along += [(2 * i + 1, (2 * i - 1) % 32) for i in range(16)]
    pairs = jnp.concatenate([pair[: 8 * size], pair_far, pair[8 * size :]])
    own_third = lax.ppermute(pairs, ("z", "xh"), along)

    own = jnp.concatenate([near, near_far, pair[: 8 * size], pair_far])
    other = lax.ppermute(own, "core", swap)
    other_third = lax.ppermute(own_third, "core", swap)
    bands = jnp.stack([band[0], pairs[16 * size], own_third[16 * size]]).astype(F32)
    return finish(ids, prm, bands, own, own_third, other, other_third)


def solution(mesh):
    parted = Mesh(mesh.devices.reshape(8, 2, 2, 16, 2), DEPTH + ("z", "xh"))
    rows = ("z", "xh")
    placed = (
        P(DEPTH, rows, None),
        P(),
        P(None, DEPTH),
        P(None, rows),
        P(None, DEPTH, None),
    )
    return jax.shard_map(
        shards, mesh=parted, in_specs=placed, out_specs=P(DEPTH, rows, None), check_vma=False
    )
```

```python
import functools

import jax
import jax.numpy as jnp
from jax import lax
from jax.experimental import pallas as pl
from jax.experimental.pallas import tpu as pltpu
from jax.sharding import Mesh, PartitionSpec as P

RATE4 = 0.56
F32 = jnp.float32
BF16 = jnp.bfloat16
I32 = jnp.int32

TILE = 32
HERE = 4
VIEWS = 4
BAND = 4
LANES = 128
NC = 4096
SIZE = VIEWS * TILE
TILES = NC // LANES // 2
SPAN = 3 * VIEWS * TILE
ROWS = 40
DEEP = HERE + 4
BATCH = 16
DEPTH = ("y", "xl", "core")


def half_conduct(diff):
    return diff / (diff * diff + 4.0)


def interpolation(ids, prm_ref, here, pair, away):
    depth, tile, xh = ids[0], ids[1], ids[2]
    lane = lax.broadcasted_iota(I32, (1, LANES), 1)
    col = lax.broadcasted_iota(I32, (1, SPAN), 1)
    view_of_col = (col >> 5) & 3
    lane_c = lax.broadcasted_iota(I32, (LANES, SPAN), 0)
    view_c = (lax.broadcasted_iota(I32, (LANES, SPAN), 1) >> 5) & 3

    row = lax.broadcasted_iota(I32, (ROWS, 1), 0)
    row = tile * TILE + jnp.where(row < 36, row, row - ROWS)
    last = 32 * TILE - 1
    row = jnp.where(row < 0, -1 - row, jnp.where(row > last, 2 * last + 1 - row, row))
    row_tile = row >> 5
    first_half = xh == 0
    before = jnp.where(first_half, away, pair)
    after = jnp.where(first_half, pair, away)
    picked = jnp.where(row_tile == tile, here, jnp.where(row_tile < tile, before, after))
    picked = jnp.where((lane & 31) == (row & 31), picked, 0.0).astype(BF16)
    same_view = ((lane_c >> 5) == view_c).astype(F32).astype(BF16)
    bands = jnp.dot(picked, same_view, preferred_element_type=F32)

    slot = col >> 7
    third = jnp.where(first_half, tile - 1, tile + 1)
    pair = jnp.where(first_half, tile + 1, tile - 1)
    source = jnp.where(slot == 0, tile, jnp.where(slot == 1, pair, third))
    col_row = jnp.where((source >= 0) & (source < 32), source * TILE + (col & 31), -100000)
    reach = (col_row - row).astype(F32) - bands

    rest = lane - 4 * VIEWS
    lane_slice = jnp.where(rest < 0, lane & 3, (rest >> 2) & 3)
    rest_c = lane_c - 4 * VIEWS
    lane_view = jnp.where(rest_c < 0, lane_c >> 2, rest_c >> 4)
    last_slice = 32 * HERE - 1
    kinds = [rest < 0] + [(rest >= 0) & (rest < 64) & ((rest & 3) == k) for k in range(BAND)]
    held = []
    for i in range(DEEP):
        at = depth * HERE + (i - 2)
        at = jnp.where(at < 0, -1 - at, jnp.where(at > last_slice, 2 * last_slice + 1 - at, at))
        mine = prm_ref[pl.ds(at >> 2, 1), :]
        held.append(jnp.where(lane_slice == (at & 3), mine, 0.0))
    held = jnp.concatenate(held, axis=0)
    stacked = jnp.concatenate([jnp.where(kind, held, 0.0) for kind in kinds], axis=0)
    spread = ((lane_view == view_c) & (rest_c < 64)).astype(F32).astype(BF16)
    table = jnp.dot(stacked.astype(BF16), spread, preferred_element_type=F32)

    parts = []
    for i in range(DEEP):
        gap = reach - table[i : i + 1, :]
        weight = jnp.zeros((ROWS, SPAN), F32)
        for k in range(BAND):
            at = (k + 1) * DEEP + i
            weight = jnp.where(gap == float(k), table[at : at + 1, :], weight)
        parts.append(weight)
    return jnp.concatenate(parts, axis=0).astype(BF16)


def sweep(src, flow, count, rows, tiles, store):
    lane = lax.broadcasted_iota(I32, (rows, LANES), 1)
    first, last = lane == 0, lane == LANES - 1

    def at(t):
        return slice(t * LANES, (t + 1) * LANES)

    for t in range(tiles):
        flow[:rows, at(t)] = half_conduct(src[1, :rows, at(t)] - src[0, :rows, at(t)])

    def one(i, carry):
        came = 0.0
        for t0 in range(0, tiles, BATCH):
            batch = range(t0, min(t0 + BATCH, tiles))
            tall = [src[i + 1, :, at(t)] for t in batch]
            ahead = [src[i + 2, :rows, at(t)] for t in batch]
            behind = [flow[:rows, at(t)] for t in batch]
            centre = [x[:rows] for x in tall]
            turned = [pltpu.roll(x, LANES - 1, 1) for x in centre]
            if t0 + BATCH < tiles:
                turned.append(pltpu.roll(src[i + 1, :rows, at(t0 + BATCH)], LANES - 1, 1))
            ahead = [half_conduct(x - c) for x, c in zip(ahead, centre)]
            total = [x - y for x, y in zip(ahead, behind)]
            step = [half_conduct(pltpu.roll(x, ROWS - 1, 0) - x) for x in tall]
            step = [(x - pltpu.roll(x, 1, 0))[:rows] for x in step]
            total = [x + y for x, y in zip(total, step)]
            step = []
            for n in range(len(batch)):
                if n + 1 < len(turned):
                    right = jnp.where(last, turned[n + 1], turned[n])
                    step.append(half_conduct(right - centre[n]))
                else:
                    step.append(jnp.where(last, 0.0, half_conduct(turned[n] - centre[n])))
            goes = [pltpu.roll(x, 1, 1) for x in step]
            total = [x + y for x, y in zip(total, step)]
            left = [jnp.where(first, x, y) for x, y in zip([came] + goes, goes)]
            came = goes[-1]
            total = [c + RATE4 * (x - y) for c, x, y in zip(centre, total, left)]
            for n, t in enumerate(batch):
                flow[:rows, at(t)] = ahead[n]
            for n, t in enumerate(batch):
                store(i, at(t), total[n])
        return carry

    lax.fori_loop(0, count, one, 0)


def half(second, ids, prm_ref, band_ref, own_ref, own_a_ref, own_b_ref, *rest):
    if second:
        other_ref, other_a_ref, other_b_ref, _, out_ref, weights, v0, v1, flow, done, sems = rest
    else:
        out_ref, weights, v0, v1, flow, done, sems = rest
    xh, core = ids[2], ids[3]
    tiles = TILES + 2 if second else TILES

    def band(ref):
        return ref[8 * SIZE :, :].astype(F32)[:1, :]

    pair_band = band(own_ref.at[2 * (1 - xh)])
    weights[...] = interpolation(ids, prm_ref, band_ref[...], pair_band, band(own_a_ref))

    def project(pieces, third, x, y, count, first):
        columns = []
        for i in range(count):
            at = pl.ds(pl.multiple_of((y + i) * SIZE, SIZE), SIZE)
            near = pieces[2 * xh + x, at, :]
            columns.append(
                jnp.concatenate([near, pieces[2 * (1 - xh) + x, at, :], third(at)], axis=0)
            )
        found = jnp.dot(
            weights[...], jnp.concatenate(columns, axis=1), preferred_element_type=F32
        )
        where = pl.ds(pl.multiple_of(first * LANES, LANES), count * LANES)
        v0[:, :, where] = found.reshape(DEEP, ROWS, count * LANES)

    if second:
        before = (1 - core) * 2
        project(other_ref, lambda at: other_a_ref[at, :], 0, 0, 8, before)
        project(other_ref, lambda at: other_b_ref[at, :], 1, 0, 8, before + 8)
        edge = jnp.where(core == 0, 0, TILES)
        project(
            own_ref,
            lambda at: jnp.where(core == 0, own_b_ref[at, :], own_a_ref[at, :]),
            1 - core,
            6 * (1 - core),
            2,
            edge,
        )
    else:
        project(own_ref, lambda at: own_a_ref[at, :], 0, 0, 8, 0)
        project(own_ref, lambda at: own_b_ref[at, :], 1, 0, 8, 8)

    def keep(i, at, value):
        v1[i, :, at] = value

    sweep(v0, flow, HERE + 2, ROWS, tiles, keep)

    count = (tiles - 1 if second else tiles) * LANES
    source, target = 0, pl.multiple_of(core * (NC // 2), LANES)
    if second:
        source = pl.multiple_of((1 - core) * LANES, LANES)
        target = pl.multiple_of((1 - core) * (TILES - 1) * LANES, LANES)

    def copy(i):
        return pltpu.make_async_copy(
            done.at[i, :, pl.ds(source, count)],
            out_ref.at[i, :, pl.ds(target, count)],
            sems.at[i],
        )

    def put(i, at, value):
        done[i, :, at] = value
        if at.stop == tiles * LANES:
            copy(i).start()

    sweep(v1, flow, HERE, TILE, tiles, put)
    for i in range(HERE):
        copy(i).wait()


def smooth(second, *operands):
    wide = (TILES + 2 if second else TILES) * LANES
    whole = pl.BlockSpec(memory_space=pltpu.VMEM)
    specs = [pl.BlockSpec(memory_space=pltpu.SMEM)] + [whole] * (8 if second else 5)
    if second:
        specs.append(pl.BlockSpec(memory_space=pl.ANY))
    return pl.pallas_call(
        functools.partial(half, second),
        out_shape=jax.ShapeDtypeStruct((HERE, TILE, NC), F32),
        in_specs=specs,
        out_specs=pl.BlockSpec(memory_space=pl.ANY),
        scratch_shapes=[
            pltpu.VMEM((DEEP * ROWS, SPAN), BF16),
            pltpu.VMEM((DEEP, ROWS, wide), F32),
            pltpu.VMEM((HERE + 2, ROWS, wide), F32),
            pltpu.VMEM((ROWS, wide), F32),
            pltpu.VMEM((HERE, TILE, wide), F32),
            pltpu.SemaphoreType.DMA((HERE,)),
        ],
        input_output_aliases={9: 0} if second else {},
        cost_estimate=pl.CostEstimate(
            flops=2 * DEEP * ROWS * SPAN * wide,
            bytes_accessed=24 * 1024 * 1024,
            transcendentals=0,
        ),
        compiler_params=pltpu.CompilerParams(vmem_limit_bytes=24 * 1024 * 1024),
    )(*operands)


def pack(stored_ref, offset_ref, taps_ref, out_ref):
    lane = lax.broadcasted_iota(I32, (1, LANES), 1)
    rest = lane - 4 * VIEWS
    line = lax.broadcasted_iota(I32, (HERE, LANES), 0)
    pick = (line == (lane & 3)).astype(F32)
    spread = jnp.dot(offset_ref[...].astype(F32), pick, preferred_element_type=F32)
    mine = (line == (lane >> 2)) & (lane < 4 * VIEWS)
    numbers = jnp.sum(jnp.where(mine, spread, 0.0), axis=0, keepdims=True)
    for v in range(VIEWS):
        spread = jnp.dot(taps_ref[v].astype(F32), pick, preferred_element_type=F32)
        mine = (line == ((rest >> 2) & 3)) & (rest >= 0) & ((rest >> 4) == v)
        numbers += jnp.sum(jnp.where(mine, spread, 0.0), axis=0, keepdims=True)
    numbers = jnp.broadcast_to(numbers, (8, LANES)).astype(BF16)
    for y in range(8):
        for xl in range(2):
            for core in range(2):
                at = ((core * 2 + xl) * 8 + y) * LANES
                piece = stored_ref[:, at : at + LANES]
                out_ref[(y * 2 + xl) * 2 + core] = jnp.concatenate([piece, numbers], axis=0)


def shards(projections, owner, row_offset, band_start, taps):
    xh, core = lax.axis_index("xh"), lax.axis_index("core")
    depth, tile = lax.axis_index(DEPTH), lax.axis_index(("z", "xh"))
    ids = jnp.stack([depth, tile, xh, core]).astype(I32)

    whole = pl.BlockSpec(memory_space=pltpu.VMEM)
    pieces = pl.pallas_call(
        pack,
        out_shape=jax.ShapeDtypeStruct((32, TILE + 8, LANES), BF16),
        in_specs=[whole] * 3,
        out_specs=whole,
    )(projections[0], row_offset, taps)
    got = lax.all_to_all(pieces, DEPTH, 0, 0, tiled=True)
    prm = got[:, TILE, :].astype(F32)
    views = jnp.concatenate(
        [lax.dynamic_index_in_dim(got, owner[v], keepdims=False)[:TILE] for v in range(VIEWS)]
    )

    near = lax.all_to_all(jnp.broadcast_to(views[None], (8, SIZE, LANES)), "y", 0, 0, tiled=True)

    band = band_start.astype(BF16).reshape(1, SIZE)
    near = jnp.concatenate([near.reshape(8 * SIZE, LANES), jnp.pad(band, ((0, 15), (0, 0)))])
    own = lax.all_to_all(
        jnp.broadcast_to(near[None], (4,) + near.shape), ("xh", "xl"), 0, 0, tiled=True
    )

    along = [(2 * i, (2 * i + 2) % 32) for i in range(16)]
    along += [(2 * i + 1, (2 * i - 1) % 32) for i in range(16)]
    pair = [lax.dynamic_index_in_dim(own, 2 * (1 - xh) + x, keepdims=False) for x in range(2)]
    thirds = [lax.ppermute(p, ("z", "xh"), along) for p in pair]

    swap = [(0, 1), (1, 0)]
    later, thirds[0] = lax.optimization_barrier((own, thirds[0]))
    other = lax.ppermute(later, "core", swap)
    other_thirds = [lax.ppermute(t, "core", swap) for t in thirds]
    first = smooth(False, ids, prm, band.astype(F32), own, *thirds)
    return smooth(True, ids, prm, band.astype(F32), own, *thirds, other, *other_thirds, first)


def solution(mesh):
    parted = Mesh(mesh.devices.reshape(8, 2, 2, 16, 2), DEPTH + ("z", "xh"))
    rows = ("z", "xh")
    placed = (
        P(DEPTH, rows, None),
        P(),
        P(None, DEPTH),
        P(None, rows),
        P(None, DEPTH, None),
    )
    return jax.shard_map(
        shards, mesh=parted, in_specs=placed, out_specs=P(DEPTH, rows, None), check_vma=False
    )
```

```python
import functools

import jax
import jax.numpy as jnp
from jax import lax
from jax.experimental import pallas as pl
from jax.experimental.pallas import tpu as pltpu
from jax.sharding import Mesh, PartitionSpec as P

RATE4 = 0.56
F32 = jnp.float32
BF16 = jnp.bfloat16
I32 = jnp.int32

TILE = 32
HERE = 4
VIEWS = 4
BAND = 4
LANES = 128
NC = 4096
SIZE = VIEWS * TILE
TILES = NC // LANES // 2
SPAN = 3 * VIEWS * TILE
ROWS = 40
DEEP = HERE + 4
BATCH = 16
DEPTH = ("y", "xl", "core")


def half_conduct(diff):
    return diff / (diff * diff + 4.0)


def interpolation(ids, prm_ref, here, pair, away):
    depth, tile, xh = ids[0], ids[1], ids[2]
    lane = lax.broadcasted_iota(I32, (1, LANES), 1)
    col = lax.broadcasted_iota(I32, (1, SPAN), 1)
    view_of_col = (col >> 5) & 3
    lane_c = lax.broadcasted_iota(I32, (LANES, SPAN), 0)
    view_c = (lax.broadcasted_iota(I32, (LANES, SPAN), 1) >> 5) & 3

    row = lax.broadcasted_iota(I32, (ROWS, 1), 0)
    row = tile * TILE + jnp.where(row < 36, row, row - ROWS)
    last = 32 * TILE - 1
    row = jnp.where(row < 0, -1 - row, jnp.where(row > last, 2 * last + 1 - row, row))
    row_tile = row >> 5
    first_half = xh == 0
    before = jnp.where(first_half, away, pair)
    after = jnp.where(first_half, pair, away)
    picked = jnp.where(row_tile == tile, here, jnp.where(row_tile < tile, before, after))
    picked = jnp.where((lane & 31) == (row & 31), picked, 0.0).astype(BF16)
    same_view = ((lane_c >> 5) == view_c).astype(F32).astype(BF16)
    bands = jnp.dot(picked, same_view, preferred_element_type=F32)

    slot = col >> 7
    third = jnp.where(first_half, tile - 1, tile + 1)
    pair = jnp.where(first_half, tile + 1, tile - 1)
    source = jnp.where(slot == 0, tile, jnp.where(slot == 1, pair, third))
    col_row = jnp.where((source >= 0) & (source < 32), source * TILE + (col & 31), -100000)
    reach = (col_row - row).astype(F32) - bands

    rest = lane - 4 * VIEWS
    lane_slice = jnp.where(rest < 0, lane & 3, (rest >> 2) & 3)
    rest_c = lane_c - 4 * VIEWS
    lane_view = jnp.where(rest_c < 0, lane_c >> 2, rest_c >> 4)
    last_slice = 32 * HERE - 1
    kinds = [rest < 0] + [(rest >= 0) & (rest < 64) & ((rest & 3) == k) for k in range(BAND)]
    held = []
    for i in range(DEEP):
        at = depth * HERE + (i - 2)
        at = jnp.where(at < 0, -1 - at, jnp.where(at > last_slice, 2 * last_slice + 1 - at, at))
        mine = prm_ref[pl.ds(at >> 2, 1), :]
        held.append(jnp.where(lane_slice == (at & 3), mine, 0.0))
    held = jnp.concatenate(held, axis=0)
    stacked = jnp.concatenate([jnp.where(kind, held, 0.0) for kind in kinds], axis=0)
    spread = ((lane_view == view_c) & (rest_c < 64)).astype(F32).astype(BF16)
    table = jnp.dot(stacked.astype(BF16), spread, preferred_element_type=F32)

    parts = []
    for i in range(DEEP):
        gap = reach - table[i : i + 1, :]
        weight = jnp.zeros((ROWS, SPAN), F32)
        for k in range(BAND):
            at = (k + 1) * DEEP + i
            weight = jnp.where(gap == float(k), table[at : at + 1, :], weight)
        parts.append(weight)
    return jnp.concatenate(parts, axis=0).astype(BF16)


def sweep(src, flow, count, rows, tiles, store):
    lane = lax.broadcasted_iota(I32, (rows, LANES), 1)
    first, last = lane == 0, lane == LANES - 1

    def at(t):
        return slice(t * LANES, (t + 1) * LANES)

    for t in range(tiles):
        flow[:rows, at(t)] = half_conduct(src[1, :rows, at(t)] - src[0, :rows, at(t)])

    def one(i, carry):
        came = 0.0
        for t0 in range(0, tiles, BATCH):
            batch = range(t0, min(t0 + BATCH, tiles))
            tall = [src[i + 1, :, at(t)] for t in batch]
            ahead = [src[i + 2, :rows, at(t)] for t in batch]
            behind = [flow[:rows, at(t)] for t in batch]
            centre = [x[:rows] for x in tall]
            turned = [pltpu.roll(x, LANES - 1, 1) for x in centre]
            if t0 + BATCH < tiles:
                turned.append(pltpu.roll(src[i + 1, :rows, at(t0 + BATCH)], LANES - 1, 1))
            ahead = [half_conduct(x - c) for x, c in zip(ahead, centre)]
            total = [x - y for x, y in zip(ahead, behind)]
            step = [half_conduct(pltpu.roll(x, ROWS - 1, 0) - x) for x in tall]
            step = [(x - pltpu.roll(x, 1, 0))[:rows] for x in step]
            total = [x + y for x, y in zip(total, step)]
            step = []
            for n in range(len(batch)):
                if n + 1 < len(turned):
                    right = jnp.where(last, turned[n + 1], turned[n])
                    step.append(half_conduct(right - centre[n]))
                else:
                    step.append(jnp.where(last, 0.0, half_conduct(turned[n] - centre[n])))
            goes = [pltpu.roll(x, 1, 1) for x in step]
            total = [x + y for x, y in zip(total, step)]
            left = [jnp.where(first, x, y) for x, y in zip([came] + goes, goes)]
            came = goes[-1]
            total = [c + RATE4 * (x - y) for c, x, y in zip(centre, total, left)]
            for n, t in enumerate(batch):
                flow[:rows, at(t)] = ahead[n]
            for n, t in enumerate(batch):
                store(i, at(t), total[n])
        return carry

    lax.fori_loop(0, count, one, 0)


def half(second, ids, prm_ref, band_ref, own_ref, *rest):
    if second:
        other_ref, _, out_ref, weights, v0, v1, flow, done, sems = rest
    else:
        out_ref, weights, v0, v1, flow, done, sems = rest
    xh, core, xl = ids[2], ids[3], ids[4]
    tiles = TILES + 2 if second else TILES

    def band(ref):
        return ref[8 * SIZE :, :].astype(F32)[:1, :]

    pair_band = band(own_ref.at[2 * (1 - xh)])
    weights[...] = interpolation(ids, prm_ref, band_ref[...], pair_band, band(own_ref.at[4]))

    def project(pieces, x, y, count, first):
        columns = []
        for i in range(count):
            at = pl.ds(pl.multiple_of((y + i) * SIZE, SIZE), SIZE)
            near = pieces[2 * xh + x, at, :]
            pair = pieces[2 * (1 - xh) + x, at, :]
            third = pieces[4 + (x ^ xl), at, :]
            columns.append(jnp.concatenate([near, pair, third], axis=0))
        found = jnp.dot(
            weights[...], jnp.concatenate(columns, axis=1), preferred_element_type=F32
        )
        where = pl.ds(pl.multiple_of(first * LANES, LANES), count * LANES)
        v0[:, :, where] = found.reshape(DEEP, ROWS, count * LANES)

    if second:
        before = (1 - core) * 2
        project(other_ref, 0, 0, 8, before)
        project(other_ref, 1, 0, 8, before + 8)
        project(own_ref, 1 - core, 6 * (1 - core), 2, core * TILES)
    else:
        project(own_ref, 0, 0, 8, 0)
        project(own_ref, 1, 0, 8, 8)

    def keep(i, at, value):
        v1[i, :, at] = value

    sweep(v0, flow, HERE + 2, ROWS, tiles, keep)

    count = (tiles - 1 if second else tiles) * LANES
    source, target = 0, pl.multiple_of(core * (NC // 2), LANES)
    if second:
        source = pl.multiple_of((1 - core) * LANES, LANES)
        target = pl.multiple_of((1 - core) * (TILES - 1) * LANES, LANES)

    def copy(i):
        return pltpu.make_async_copy(
            done.at[i, :, pl.ds(source, count)],
            out_ref.at[i, :, pl.ds(target, count)],
            sems.at[i],
        )

    def put(i, at, value):
        done[i, :, at] = value
        if at.stop == tiles * LANES:
            copy(i).start()

    sweep(v1, flow, HERE, TILE, tiles, put)
    for i in range(HERE):
        copy(i).wait()


def smooth(second, *operands):
    wide = (TILES + 2 if second else TILES) * LANES
    whole = pl.BlockSpec(memory_space=pltpu.VMEM)
    specs = [pl.BlockSpec(memory_space=pltpu.SMEM)] + [whole] * (4 if second else 3)
    if second:
        specs.append(pl.BlockSpec(memory_space=pl.ANY))
    return pl.pallas_call(
        functools.partial(half, second),
        out_shape=jax.ShapeDtypeStruct((HERE, TILE, NC), F32),
        in_specs=specs,
        out_specs=pl.BlockSpec(memory_space=pl.ANY),
        scratch_shapes=[
            pltpu.VMEM((DEEP * ROWS, SPAN), BF16),
            pltpu.VMEM((DEEP, ROWS, wide), F32),
            pltpu.VMEM((HERE + 2, ROWS, wide), F32),
            pltpu.VMEM((ROWS, wide), F32),
            pltpu.VMEM((HERE, TILE, wide), F32),
            pltpu.SemaphoreType.DMA((HERE,)),
        ],
        input_output_aliases={5: 0} if second else {},
        cost_estimate=pl.CostEstimate(
            flops=2 * DEEP * ROWS * SPAN * wide,
            bytes_accessed=24 * 1024 * 1024,
            transcendentals=0,
        ),
        compiler_params=pltpu.CompilerParams(vmem_limit_bytes=24 * 1024 * 1024),
    )(*operands)


def pack(stored_ref, offset_ref, taps_ref, out_ref):
    lane = lax.broadcasted_iota(I32, (1, LANES), 1)
    rest = lane - 4 * VIEWS
    line = lax.broadcasted_iota(I32, (HERE, LANES), 0)
    pick = (line == (lane & 3)).astype(F32)
    spread = jnp.dot(offset_ref[...].astype(F32), pick, preferred_element_type=F32)
    mine = (line == (lane >> 2)) & (lane < 4 * VIEWS)
    numbers = jnp.sum(jnp.where(mine, spread, 0.0), axis=0, keepdims=True)
    for v in range(VIEWS):
        spread = jnp.dot(taps_ref[v].astype(F32), pick, preferred_element_type=F32)
        mine = (line == ((rest >> 2) & 3)) & (rest >= 0) & ((rest >> 4) == v)
        numbers += jnp.sum(jnp.where(mine, spread, 0.0), axis=0, keepdims=True)
    numbers = jnp.broadcast_to(numbers, (8, LANES)).astype(BF16)
    for y in range(8):
        for xl in range(2):
            for core in range(2):
                at = ((core * 2 + xl) * 8 + y) * LANES
                piece = stored_ref[:, at : at + LANES]
                out_ref[(y * 2 + xl) * 2 + core] = jnp.concatenate([piece, numbers], axis=0)


def shards(projections, owner, row_offset, band_start, taps):
    xh, xl, core = (lax.axis_index(a) for a in ("xh", "xl", "core"))
    depth, tile = lax.axis_index(DEPTH), lax.axis_index(("z", "xh"))
    ids = jnp.stack([depth, tile, xh, core, xl]).astype(I32)

    whole = pl.BlockSpec(memory_space=pltpu.VMEM)
    pieces = pl.pallas_call(
        pack,
        out_shape=jax.ShapeDtypeStruct((32, TILE + 8, LANES), BF16),
        in_specs=[whole] * 3,
        out_specs=whole,
    )(projections[0], row_offset, taps)
    got = lax.all_to_all(pieces, DEPTH, 0, 0, tiled=True)
    prm = got[:, TILE, :].astype(F32)
    views = jnp.concatenate(
        [lax.dynamic_index_in_dim(got, owner[v], keepdims=False)[:TILE] for v in range(VIEWS)]
    )

    band = band_start.astype(BF16).reshape(1, SIZE)
    rest = (band.astype(F32), jnp.pad(band, ((0, 15), (0, 0))), prm, ids)
    views, (band, band_rows, prm, ids) = lax.optimization_barrier((views, rest))
    near = lax.all_to_all(jnp.broadcast_to(views[None], (8, SIZE, LANES)), "y", 0, 0, tiled=True)
    near = jnp.concatenate([near.reshape(8 * SIZE, LANES), band_rows])

    shift = [(2 * i, (2 * i - 2) % 32) for i in range(16)]
    shift += [(2 * i + 1, (2 * i + 3) % 32) for i in range(16)]
    foreign = lax.ppermute(near, ("z", "xh"), shift)
    own = lax.all_to_all(
        jnp.broadcast_to(near[None], (4,) + near.shape), ("xh", "xl"), 0, 0, tiled=True
    )

    own, foreign = lax.optimization_barrier((own, foreign))

    along = [(a, b) for b, a in shift]
    third = lax.dynamic_index_in_dim(own, 2 * (1 - xh) + xl, keepdims=False)
    third = lax.ppermute(third, ("z", "xh"), along)
    third_far = lax.ppermute(foreign, ("xl", "xh"), [(0, 3), (1, 2), (2, 1), (3, 0)])

    swap = [(0, 1), (1, 0)]
    own = jnp.concatenate([own, third[None], third_far[None]])
    other = lax.ppermute(own, "core", swap)
    first = smooth(False, ids, prm, band, own)
    return smooth(True, ids, prm, band, own, other, first)


def solution(mesh):
    parted = Mesh(mesh.devices.reshape(8, 2, 2, 16, 2), DEPTH + ("z", "xh"))
    rows = ("z", "xh")
    placed = (
        P(DEPTH, rows, None),
        P(),
        P(None, DEPTH),
        P(None, rows),
        P(None, DEPTH, None),
    )
    return jax.shard_map(
        shards, mesh=parted, in_specs=placed, out_specs=P(DEPTH, rows, None), check_vma=False
    )
```

```python
import functools

import jax
import jax.numpy as jnp
from jax import lax
from jax.experimental import pallas as pl
from jax.experimental.pallas import tpu as pltpu
from jax.sharding import Mesh, PartitionSpec as P

RATE4 = 0.56
F32 = jnp.float32
BF16 = jnp.bfloat16
I32 = jnp.int32

TILE = 32
HERE = 4
VIEWS = 4
BAND = 4
LANES = 128
NC = 4096
SIZE = VIEWS * TILE
TILES = NC // LANES // 2
SPAN = 3 * VIEWS * TILE
ROWS = 40
DEEP = HERE + 4
BATCH = 16
DEPTH = ("y", "xl", "core")


def half_conduct(diff):
    return diff / (diff * diff + 4.0)


def interpolation(ids, prm_ref, here, pair, away):
    depth, tile, xh = ids[0], ids[1], ids[2]
    lane = lax.broadcasted_iota(I32, (1, LANES), 1)
    col = lax.broadcasted_iota(I32, (1, SPAN), 1)
    view_of_col = (col >> 5) & 3
    lane_c = lax.broadcasted_iota(I32, (LANES, SPAN), 0)
    view_c = (lax.broadcasted_iota(I32, (LANES, SPAN), 1) >> 5) & 3

    row = lax.broadcasted_iota(I32, (ROWS, 1), 0)
    row = tile * TILE + jnp.where(row < 36, row, row - ROWS)
    last = 32 * TILE - 1
    row = jnp.where(row < 0, -1 - row, jnp.where(row > last, 2 * last + 1 - row, row))
    row_tile = row >> 5
    first_half = xh == 0
    before = jnp.where(first_half, away, pair)
    after = jnp.where(first_half, pair, away)
    picked = jnp.where(row_tile == tile, here, jnp.where(row_tile < tile, before, after))
    picked = jnp.where((lane & 31) == (row & 31), picked, 0.0).astype(BF16)
    same_view = ((lane_c >> 5) == view_c).astype(F32).astype(BF16)
    bands = jnp.dot(picked, same_view, preferred_element_type=F32)

    slot = col >> 7
    third = jnp.where(first_half, tile - 1, tile + 1)
    pair = jnp.where(first_half, tile + 1, tile - 1)
    source = jnp.where(slot == 0, tile, jnp.where(slot == 1, pair, third))
    col_row = jnp.where((source >= 0) & (source < 32), source * TILE + (col & 31), -100000)
    reach = (col_row - row).astype(F32) - bands

    rest = lane - 4 * VIEWS
    lane_slice = jnp.where(rest < 0, lane & 3, (rest >> 2) & 3)
    rest_c = lane_c - 4 * VIEWS
    lane_view = jnp.where(rest_c < 0, lane_c >> 2, rest_c >> 4)
    last_slice = 32 * HERE - 1
    kinds = [rest < 0] + [(rest >= 0) & (rest < 64) & ((rest & 3) == k) for k in range(BAND)]
    held = []
    for i in range(DEEP):
        at = depth * HERE + (i - 2)
        at = jnp.where(at < 0, -1 - at, jnp.where(at > last_slice, 2 * last_slice + 1 - at, at))
        mine = prm_ref[pl.ds((at >> 2) - depth + 1, 1), :]
        held.append(jnp.where(lane_slice == (at & 3), mine, 0.0))
    held = jnp.concatenate(held, axis=0)
    stacked = jnp.concatenate([jnp.where(kind, held, 0.0) for kind in kinds], axis=0)
    spread = ((lane_view == view_c) & (rest_c < 64)).astype(F32).astype(BF16)
    table = jnp.dot(stacked.astype(BF16), spread, preferred_element_type=F32)

    parts = []
    for i in range(DEEP):
        gap = reach - table[i : i + 1, :]
        weight = jnp.zeros((ROWS, SPAN), F32)
        for k in range(BAND):
            at = (k + 1) * DEEP + i
            weight = jnp.where(gap == float(k), table[at : at + 1, :], weight)
        parts.append(weight)
    return jnp.concatenate(parts, axis=0).astype(BF16)


def sweep(src, flow, count, rows, tiles, store):
    lane = lax.broadcasted_iota(I32, (rows, LANES), 1)
    first, last = lane == 0, lane == LANES - 1

    def at(t):
        return slice(t * LANES, (t + 1) * LANES)

    for t in range(tiles):
        flow[:rows, at(t)] = half_conduct(src[1, :rows, at(t)] - src[0, :rows, at(t)])

    def one(i, carry):
        came = 0.0
        for t0 in range(0, tiles, BATCH):
            batch = range(t0, min(t0 + BATCH, tiles))
            tall = [src[i + 1, :, at(t)] for t in batch]
            ahead = [src[i + 2, :rows, at(t)] for t in batch]
            behind = [flow[:rows, at(t)] for t in batch]
            centre = [x[:rows] for x in tall]
            turned = [pltpu.roll(x, LANES - 1, 1) for x in centre]
            if t0 + BATCH < tiles:
                turned.append(pltpu.roll(src[i + 1, :rows, at(t0 + BATCH)], LANES - 1, 1))
            ahead = [half_conduct(x - c) for x, c in zip(ahead, centre)]
            total = [x - y for x, y in zip(ahead, behind)]
            step = [half_conduct(pltpu.roll(x, ROWS - 1, 0) - x) for x in tall]
            step = [(x - pltpu.roll(x, 1, 0))[:rows] for x in step]
            total = [x + y for x, y in zip(total, step)]
            step = []
            for n in range(len(batch)):
                if n + 1 < len(turned):
                    right = jnp.where(last, turned[n + 1], turned[n])
                    step.append(half_conduct(right - centre[n]))
                else:
                    step.append(jnp.where(last, 0.0, half_conduct(turned[n] - centre[n])))
            goes = [pltpu.roll(x, 1, 1) for x in step]
            total = [x + y for x, y in zip(total, step)]
            left = [jnp.where(first, x, y) for x, y in zip([came] + goes, goes)]
            came = goes[-1]
            total = [c + RATE4 * (x - y) for c, x, y in zip(centre, total, left)]
            for n, t in enumerate(batch):
                flow[:rows, at(t)] = ahead[n]
            for n, t in enumerate(batch):
                store(i, at(t), total[n])
        return carry

    lax.fori_loop(0, count, one, 0)


def half(second, ids, prm_ref, band_ref, own_ref, *rest):
    if second:
        other_ref, _, out_ref, weights, v0, v1, flow, done, sems = rest
    else:
        out_ref, weights, v0, v1, flow, done, sems = rest
    xh, core, xl = ids[2], ids[3], ids[4]
    tiles = TILES + 2 if second else TILES

    def band(ref):
        return ref[8 * SIZE :, :].astype(F32)[:1, :]

    pair_band = band(own_ref.at[2 * (1 - xh)])
    weights[...] = interpolation(ids, prm_ref, band_ref[...], pair_band, band(own_ref.at[4]))

    def project(pieces, x, y, count, first):
        columns = []
        for i in range(count):
            at = pl.ds(pl.multiple_of((y + i) * SIZE, SIZE), SIZE)
            near = pieces[2 * xh + x, at, :]
            pair = pieces[2 * (1 - xh) + x, at, :]
            third = pieces[4 + (x ^ xl), at, :]
            columns.append(jnp.concatenate([near, pair, third], axis=0))
        found = jnp.dot(
            weights[...], jnp.concatenate(columns, axis=1), preferred_element_type=F32
        )
        where = pl.ds(pl.multiple_of(first * LANES, LANES), count * LANES)
        v0[:, :, where] = found.reshape(DEEP, ROWS, count * LANES)

    if second:
        before = (1 - core) * 2
        project(other_ref, 0, 0, 8, before)
        project(other_ref, 1, 0, 8, before + 8)
        project(own_ref, 1 - core, 6 * (1 - core), 2, core * TILES)
    else:
        project(own_ref, 0, 0, 8, 0)
        project(own_ref, 1, 0, 8, 8)

    def keep(i, at, value):
        v1[i, :, at] = value

    sweep(v0, flow, HERE + 2, ROWS, tiles, keep)

    count = (tiles - 1 if second else tiles) * LANES
    source, target = 0, pl.multiple_of(core * (NC // 2), LANES)
    if second:
        source = pl.multiple_of((1 - core) * LANES, LANES)
        target = pl.multiple_of((1 - core) * (TILES - 1) * LANES, LANES)

    def copy(i):
        return pltpu.make_async_copy(
            done.at[i, :, pl.ds(source, count)],
            out_ref.at[i, :, pl.ds(target, count)],
            sems.at[i],
        )

    def put(i, at, value):
        done[i, :, at] = value
        if at.stop == tiles * LANES:
            copy(i).start()

    sweep(v1, flow, HERE, TILE, tiles, put)
    for i in range(HERE):
        copy(i).wait()


def smooth(second, *operands):
    wide = (TILES + 2 if second else TILES) * LANES
    whole = pl.BlockSpec(memory_space=pltpu.VMEM)
    specs = [pl.BlockSpec(memory_space=pltpu.SMEM)] + [whole] * (4 if second else 3)
    if second:
        specs.append(pl.BlockSpec(memory_space=pl.ANY))
    return pl.pallas_call(
        functools.partial(half, second),
        out_shape=jax.ShapeDtypeStruct((HERE, TILE, NC), F32),
        in_specs=specs,
        out_specs=pl.BlockSpec(memory_space=pl.ANY),
        scratch_shapes=[
            pltpu.VMEM((DEEP * ROWS, SPAN), BF16),
            pltpu.VMEM((DEEP, ROWS, wide), F32),
            pltpu.VMEM((HERE + 2, ROWS, wide), F32),
            pltpu.VMEM((ROWS, wide), F32),
            pltpu.VMEM((HERE, TILE, wide), F32),
            pltpu.SemaphoreType.DMA((HERE,)),
        ],
        input_output_aliases={5: 0} if second else {},
        cost_estimate=pl.CostEstimate(
            flops=2 * DEEP * ROWS * SPAN * wide,
            bytes_accessed=24 * 1024 * 1024,
            transcendentals=0,
        ),
        compiler_params=pltpu.CompilerParams(vmem_limit_bytes=24 * 1024 * 1024),
    )(*operands)


def pack(stored_ref, offset_ref, taps_ref, out_ref, numbers_ref):
    lane = lax.broadcasted_iota(I32, (1, LANES), 1)
    rest = lane - 4 * VIEWS
    line = lax.broadcasted_iota(I32, (HERE, LANES), 0)
    pick = (line == (lane & 3)).astype(F32)
    spread = jnp.dot(offset_ref[...].astype(F32), pick, preferred_element_type=F32)
    mine = (line == (lane >> 2)) & (lane < 4 * VIEWS)
    numbers = jnp.sum(jnp.where(mine, spread, 0.0), axis=0, keepdims=True)
    for v in range(VIEWS):
        spread = jnp.dot(taps_ref[v].astype(F32), pick, preferred_element_type=F32)
        mine = (line == ((rest >> 2) & 3)) & (rest >= 0) & ((rest >> 4) == v)
        numbers += jnp.sum(jnp.where(mine, spread, 0.0), axis=0, keepdims=True)
    numbers_ref[...] = jnp.broadcast_to(numbers, (16, LANES)).astype(BF16)
    for y in range(8):
        for xl in range(2):
            for core in range(2):
                at = ((core * 2 + xl) * 8 + y) * LANES
                out_ref[(y * 2 + xl) * 2 + core] = stored_ref[:, at : at + LANES]


def shards(projections, owner, row_offset, band_start, taps):
    xh, xl, core = (lax.axis_index(a) for a in ("xh", "xl", "core"))
    depth, tile = lax.axis_index(DEPTH), lax.axis_index(("z", "xh"))
    ids = jnp.stack([depth, tile, xh, core, xl]).astype(I32)

    whole = pl.BlockSpec(memory_space=pltpu.VMEM)
    pieces, numbers = pl.pallas_call(
        pack,
        out_shape=(
            jax.ShapeDtypeStruct((32, TILE, LANES), BF16),
            jax.ShapeDtypeStruct((16, LANES), BF16),
        ),
        in_specs=[whole] * 3,
        out_specs=[whole] * 2,
    )(projections[0], row_offset, taps)
    got = lax.all_to_all(pieces, DEPTH, 0, 0, tiled=True)
    views = jnp.concatenate(
        [lax.dynamic_index_in_dim(got, owner[v], keepdims=False) for v in range(VIEWS)]
    )
    lower = lax.ppermute(numbers, DEPTH, [(i, (i + 1) % 32) for i in range(32)])
    upper = lax.ppermute(numbers, DEPTH, [((i + 1) % 32, i) for i in range(32)])
    prm = jnp.concatenate([lower[:1], numbers[:1], upper[:1]]).astype(F32)

    band = band_start.astype(BF16).reshape(1, SIZE)
    rest = (band.astype(F32), jnp.pad(band, ((0, 15), (0, 0))), prm, ids)
    views, (band, band_rows, prm, ids) = lax.optimization_barrier((views, rest))
    near = lax.all_to_all(jnp.broadcast_to(views[None], (8, SIZE, LANES)), "y", 0, 0, tiled=True)
    near = jnp.concatenate([near.reshape(8 * SIZE, LANES), band_rows])

    swap = [(0, 1), (1, 0)]
    shift = [(2 * i, (2 * i - 2) % 32) for i in range(16)]
    shift += [(2 * i + 1, (2 * i + 3) % 32) for i in range(16)]
    foreign = lax.ppermute(near, ("z", "xh"), shift)
    own = lax.all_to_all(
        jnp.broadcast_to(near[None], (4,) + near.shape), ("xh", "xl"), 0, 0, tiled=True
    )

    third_far = lax.ppermute(foreign, ("xl", "xh"), [(0, 3), (1, 2), (2, 1), (3, 0)])
    third = lax.ppermute(third_far, "xl", swap)
    own, third = lax.optimization_barrier((own, third))

    own = jnp.concatenate([own, third[None], third_far[None]])
    other = lax.ppermute(own, "core", swap)
    first = smooth(False, ids, prm, band, own)
    return smooth(True, ids, prm, band, own, other, first)


def solution(mesh):
    parted = Mesh(mesh.devices.reshape(8, 2, 2, 16, 2), DEPTH + ("z", "xh"))
    rows = ("z", "xh")
    placed = (
        P(DEPTH, rows, None),
        P(),
        P(None, DEPTH),
        P(None, rows),
        P(None, DEPTH, None),
    )
    return jax.shard_map(
        shards, mesh=parted, in_specs=placed, out_specs=P(DEPTH, rows, None), check_vma=False
    )
```

```python
import functools

import jax
import jax.numpy as jnp
from jax import lax
from jax.experimental import pallas as pl
from jax.experimental.pallas import tpu as pltpu
from jax.sharding import Mesh, PartitionSpec as P

RATE4 = 0.56
F32 = jnp.float32
BF16 = jnp.bfloat16
I32 = jnp.int32

TILE = 32
HERE = 4
VIEWS = 4
BAND = 4
LANES = 128
NC = 4096
SIZE = VIEWS * TILE
TILES = NC // LANES // 2
SPAN = 3 * VIEWS * TILE
ROWS = 40
DEEP = HERE + 4
BATCH = 16
DEPTH = ("y", "xl", "core")


def half_conduct(diff):
    return diff / (diff * diff + 4.0)


def interpolation(ids, prm_ref, here, pair, away):
    depth, tile, xh = ids[0], ids[1], ids[2]
    lane = lax.broadcasted_iota(I32, (1, LANES), 1)
    col = lax.broadcasted_iota(I32, (1, SPAN), 1)
    view_of_col = (col >> 5) & 3
    lane_c = lax.broadcasted_iota(I32, (LANES, SPAN), 0)
    view_c = (lax.broadcasted_iota(I32, (LANES, SPAN), 1) >> 5) & 3

    row = lax.broadcasted_iota(I32, (ROWS, 1), 0)
    row = tile * TILE + jnp.where(row < 36, row, row - ROWS)
    last = 32 * TILE - 1
    row = jnp.where(row < 0, -1 - row, jnp.where(row > last, 2 * last + 1 - row, row))
    row_tile = row >> 5
    first_half = xh == 0
    before = jnp.where(first_half, away, pair)
    after = jnp.where(first_half, pair, away)
    picked = jnp.where(row_tile == tile, here, jnp.where(row_tile < tile, before, after))
    picked = jnp.where((lane & 31) == (row & 31), picked, 0.0).astype(BF16)
    same_view = ((lane_c >> 5) == view_c).astype(F32).astype(BF16)
    bands = jnp.dot(picked, same_view, preferred_element_type=F32)

    slot = col >> 7
    third = jnp.where(first_half, tile - 1, tile + 1)
    pair = jnp.where(first_half, tile + 1, tile - 1)
    source = jnp.where(slot == 0, tile, jnp.where(slot == 1, pair, third))
    col_row = jnp.where((source >= 0) & (source < 32), source * TILE + (col & 31), -100000)
    reach = (col_row - row).astype(F32) - bands

    rest = lane - 4 * VIEWS
    lane_slice = jnp.where(rest < 0, lane & 3, (rest >> 2) & 3)
    rest_c = lane_c - 4 * VIEWS
    lane_view = jnp.where(rest_c < 0, lane_c >> 2, rest_c >> 4)
    last_slice = 32 * HERE - 1
    kinds = [rest < 0] + [(rest >= 0) & (rest < 64) & ((rest & 3) == k) for k in range(BAND)]
    held = []
    for i in range(DEEP):
        at = depth * HERE + (i - 2)
        at = jnp.where(at < 0, -1 - at, jnp.where(at > last_slice, 2 * last_slice + 1 - at, at))
        mine = prm_ref[pl.ds(at >> 2, 1), :]
        held.append(jnp.where(lane_slice == (at & 3), mine, 0.0))
    held = jnp.concatenate(held, axis=0)
    stacked = jnp.concatenate([jnp.where(kind, held, 0.0) for kind in kinds], axis=0)
    spread = ((lane_view == view_c) & (rest_c < 64)).astype(F32).astype(BF16)
    table = jnp.dot(stacked.astype(BF16), spread, preferred_element_type=F32)

    parts = []
    for i in range(DEEP):
        gap = reach - table[i : i + 1, :]
        weight = jnp.zeros((ROWS, SPAN), F32)
        for k in range(BAND):
            at = (k + 1) * DEEP + i
            weight = jnp.where(gap == float(k), table[at : at + 1, :], weight)
        parts.append(weight)
    return jnp.concatenate(parts, axis=0).astype(BF16)


def sweep(src, flow, count, rows, tiles, store):
    lane = lax.broadcasted_iota(I32, (rows, LANES), 1)
    first, last = lane == 0, lane == LANES - 1

    def at(t):
        return slice(t * LANES, (t + 1) * LANES)

    for t in range(tiles):
        flow[:rows, at(t)] = half_conduct(src[1, :rows, at(t)] - src[0, :rows, at(t)])

    def one(i, carry):
        came = 0.0
        for t0 in range(0, tiles, BATCH):
            batch = range(t0, min(t0 + BATCH, tiles))
            tall = [src[i + 1, :, at(t)] for t in batch]
            ahead = [src[i + 2, :rows, at(t)] for t in batch]
            behind = [flow[:rows, at(t)] for t in batch]
            centre = [x[:rows] for x in tall]
            turned = [pltpu.roll(x, LANES - 1, 1) for x in centre]
            if t0 + BATCH < tiles:
                turned.append(pltpu.roll(src[i + 1, :rows, at(t0 + BATCH)], LANES - 1, 1))
            ahead = [half_conduct(x - c) for x, c in zip(ahead, centre)]
            total = [x - y for x, y in zip(ahead, behind)]
            step = [half_conduct(pltpu.roll(x, ROWS - 1, 0) - x) for x in tall]
            step = [(x - pltpu.roll(x, 1, 0))[:rows] for x in step]
            total = [x + y for x, y in zip(total, step)]
            step = []
            for n in range(len(batch)):
                if n + 1 < len(turned):
                    right = jnp.where(last, turned[n + 1], turned[n])
                    step.append(half_conduct(right - centre[n]))
                else:
                    step.append(jnp.where(last, 0.0, half_conduct(turned[n] - centre[n])))
            goes = [pltpu.roll(x, 1, 1) for x in step]
            total = [x + y for x, y in zip(total, step)]
            left = [jnp.where(first, x, y) for x, y in zip([came] + goes, goes)]
            came = goes[-1]
            total = [c + RATE4 * (x - y) for c, x, y in zip(centre, total, left)]
            for n, t in enumerate(batch):
                flow[:rows, at(t)] = ahead[n]
            for n, t in enumerate(batch):
                store(i, at(t), total[n])
        return carry

    lax.fori_loop(0, count, one, 0)


def half(second, ids, prm_ref, band_ref, own_ref, *rest):
    if second:
        other_ref, _, out_ref, weights, v0, v1, flow, done, sems = rest
    else:
        out_ref, weights, v0, v1, flow, done, sems = rest
    xh, core, xl = ids[2], ids[3], ids[4]
    tiles = TILES + 2 if second else TILES

    def band(ref):
        return ref[8 * SIZE :, :].astype(F32)[:1, :]

    pair_band = band(own_ref.at[2 * (1 - xh)])
    weights[...] = interpolation(ids, prm_ref, band_ref[...], pair_band, band(own_ref.at[4]))

    def project(pieces, x, y, count, first):
        columns = []
        for i in range(count):
            at = pl.ds(pl.multiple_of((y + i) * SIZE, SIZE), SIZE)
            near = pieces[2 * xh + x, at, :]
            pair = pieces[2 * (1 - xh) + x, at, :]
            third = pieces[4 + (x ^ xl), at, :]
            columns.append(jnp.concatenate([near, pair, third], axis=0))
        found = jnp.dot(
            weights[...], jnp.concatenate(columns, axis=1), preferred_element_type=F32
        )
        where = pl.ds(pl.multiple_of(first * LANES, LANES), count * LANES)
        v0[:, :, where] = found.reshape(DEEP, ROWS, count * LANES)

    if second:
        before = (1 - core) * 2
        project(other_ref, 0, 0, 8, before)
        project(other_ref, 1, 0, 8, before + 8)
        project(own_ref, 1 - core, 6 * (1 - core), 2, core * TILES)
    else:
        project(own_ref, 0, 0, 8, 0)
        project(own_ref, 1, 0, 8, 8)

    def keep(i, at, value):
        v1[i, :, at] = value

    sweep(v0, flow, HERE + 2, ROWS, tiles, keep)

    count = (tiles - 1 if second else tiles) * LANES
    source, target = 0, pl.multiple_of(core * (NC // 2), LANES)
    if second:
        source = pl.multiple_of((1 - core) * LANES, LANES)
        target = pl.multiple_of((1 - core) * (TILES - 1) * LANES, LANES)

    def copy(i):
        return pltpu.make_async_copy(
            done.at[i, :, pl.ds(source, count)],
            out_ref.at[i, :, pl.ds(target, count)],
            sems.at[i],
        )

    def put(i, at, value):
        done[i, :, at] = value
        if at.stop == tiles * LANES:
            copy(i).start()

    sweep(v1, flow, HERE, TILE, tiles, put)
    for i in range(HERE):
        copy(i).wait()


def smooth(second, *operands):
    wide = (TILES + 2 if second else TILES) * LANES
    whole = pl.BlockSpec(memory_space=pltpu.VMEM)
    specs = [pl.BlockSpec(memory_space=pltpu.SMEM)] + [whole] * (4 if second else 3)
    if second:
        specs.append(pl.BlockSpec(memory_space=pl.ANY))
    return pl.pallas_call(
        functools.partial(half, second),
        out_shape=jax.ShapeDtypeStruct((HERE, TILE, NC), F32),
        in_specs=specs,
        out_specs=pl.BlockSpec(memory_space=pl.ANY),
        scratch_shapes=[
            pltpu.VMEM((DEEP * ROWS, SPAN), BF16),
            pltpu.VMEM((DEEP, ROWS, wide), F32),
            pltpu.VMEM((HERE + 2, ROWS, wide), F32),
            pltpu.VMEM((ROWS, wide), F32),
            pltpu.VMEM((HERE, TILE, wide), F32),
            pltpu.SemaphoreType.DMA((HERE,)),
        ],
        input_output_aliases={5: 0} if second else {},
        cost_estimate=pl.CostEstimate(
            flops=2 * DEEP * ROWS * SPAN * wide,
            bytes_accessed=24 * 1024 * 1024,
            transcendentals=0,
        ),
        compiler_params=pltpu.CompilerParams(vmem_limit_bytes=24 * 1024 * 1024),
    )(*operands)


def pack(stored_ref, offset_ref, taps_ref, out_ref):
    lane = lax.broadcasted_iota(I32, (1, LANES), 1)
    rest = lane - 4 * VIEWS
    line = lax.broadcasted_iota(I32, (HERE, LANES), 0)
    pick = (line == (lane & 3)).astype(F32)
    spread = jnp.dot(offset_ref[...].astype(F32), pick, preferred_element_type=F32)
    mine = (line == (lane >> 2)) & (lane < 4 * VIEWS)
    numbers = jnp.sum(jnp.where(mine, spread, 0.0), axis=0, keepdims=True)
    for v in range(VIEWS):
        spread = jnp.dot(taps_ref[v].astype(F32), pick, preferred_element_type=F32)
        mine = (line == ((rest >> 2) & 3)) & (rest >= 0) & ((rest >> 4) == v)
        numbers += jnp.sum(jnp.where(mine, spread, 0.0), axis=0, keepdims=True)
    numbers = jnp.broadcast_to(numbers, (8, LANES)).astype(BF16)
    for y in range(8):
        for xl in range(2):
            for core in range(2):
                at = ((core * 2 + xl) * 8 + y) * LANES
                piece = stored_ref[:, at : at + LANES]
                out_ref[(y * 2 + xl) * 2 + core] = jnp.concatenate([piece, numbers], axis=0)


def shards(projections, owner, row_offset, band_start, taps):
    xh, xl, core = (lax.axis_index(a) for a in ("xh", "xl", "core"))
    depth, tile = lax.axis_index(DEPTH), lax.axis_index(("z", "xh"))
    ids = jnp.stack([depth, tile, xh, core, xl]).astype(I32)

    whole = pl.BlockSpec(memory_space=pltpu.VMEM)
    pieces = pl.pallas_call(
        pack,
        out_shape=jax.ShapeDtypeStruct((32, TILE + 8, LANES), BF16),
        in_specs=[whole] * 3,
        out_specs=whole,
    )(projections[0], row_offset, taps)
    got = lax.all_to_all(pieces, DEPTH, 0, 0, tiled=True)
    prm = got[:, TILE, :].astype(F32)
    views = jnp.concatenate(
        [
            lax.dynamic_slice(
                got, (owner[v], 0, 0), (1, TILE, LANES), allow_negative_indices=False
            )[0]
            for v in range(VIEWS)
        ]
    )

    band = band_start.astype(BF16).reshape(1, SIZE)
    rest = (band.astype(F32), jnp.pad(band, ((0, 15), (0, 0))), prm, ids)
    views, (band, band_rows, prm, ids) = lax.optimization_barrier((views, rest))
    near = lax.all_to_all(jnp.broadcast_to(views[None], (8, SIZE, LANES)), "y", 0, 0, tiled=True)
    near = jnp.concatenate([near.reshape(8 * SIZE, LANES), band_rows])

    shift = [(2 * i + 2, 2 * i) for i in range(15)] + [(2 * i + 1, 2 * i + 3) for i in range(15)]
    foreign = lax.ppermute(near, ("z", "xh"), shift)
    own = lax.all_to_all(
        jnp.broadcast_to(near[None], (4,) + near.shape), ("xh", "xl"), 0, 0, tiled=True
    )

    own, foreign = lax.optimization_barrier((own, foreign))

    along = [(a, b) for b, a in shift]
    third = lax.dynamic_slice(
        own, (2 * (1 - xh) + xl, 0, 0), (1,) + near.shape, allow_negative_indices=False
    )[0]
    third = lax.ppermute(third, ("z", "xh"), along)
    third_far = lax.ppermute(foreign, ("xl", "xh"), [(0, 3), (1, 2), (2, 1), (3, 0)])

    swap = [(0, 1), (1, 0)]
    own = jnp.concatenate([own, third[None], third_far[None]])
    other = lax.ppermute(own, "core", swap)
    first = smooth(False, ids, prm, band, own)
    return smooth(True, ids, prm, band, own, other, first)


def solution(mesh):
    parted = Mesh(mesh.devices.reshape(8, 2, 2, 16, 2), DEPTH + ("z", "xh"))
    rows = ("z", "xh")
    placed = (
        P(DEPTH, rows, None),
        P(),
        P(None, DEPTH),
        P(None, rows),
        P(None, DEPTH, None),
    )
    return jax.shard_map(
        shards, mesh=parted, in_specs=placed, out_specs=P(DEPTH, rows, None), check_vma=False
    )
```

```python
import functools

import jax
import jax.numpy as jnp
from jax import lax
from jax.experimental import pallas as pl
from jax.experimental.pallas import tpu as pltpu
from jax.sharding import Mesh, PartitionSpec as P

RATE4 = 0.56
F32 = jnp.float32
BF16 = jnp.bfloat16
I32 = jnp.int32

TILE = 32
HERE = 4
VIEWS = 4
BAND = 4
LANES = 128
NC = 4096
SIZE = VIEWS * TILE
TILES = NC // LANES // 2
SPAN = 3 * VIEWS * TILE
ROWS = 40
DEEP = HERE + 4
BATCH = 16
DEPTH = ("y", "xl", "core")


def half_conduct(diff):
    return diff / (diff * diff + 4.0)


def interpolation(ids, prm_ref, here, pair, away):
    depth, tile, xh = ids[0], ids[1], ids[2]
    lane = lax.broadcasted_iota(I32, (1, LANES), 1)
    col = lax.broadcasted_iota(I32, (1, SPAN), 1)
    view_of_col = (col >> 5) & 3
    lane_c = lax.broadcasted_iota(I32, (LANES, SPAN), 0)
    view_c = (lax.broadcasted_iota(I32, (LANES, SPAN), 1) >> 5) & 3

    row = lax.broadcasted_iota(I32, (ROWS, 1), 0)
    row = tile * TILE + jnp.where(row < 36, row, row - ROWS)
    last = 32 * TILE - 1
    row = jnp.where(row < 0, -1 - row, jnp.where(row > last, 2 * last + 1 - row, row))
    row_tile = row >> 5
    first_half = xh == 0
    before = jnp.where(first_half, away, pair)
    after = jnp.where(first_half, pair, away)
    picked = jnp.where(row_tile == tile, here, jnp.where(row_tile < tile, before, after))
    picked = jnp.where((lane & 31) == (row & 31), picked, 0.0).astype(BF16)
    same_view = ((lane_c >> 5) == view_c).astype(F32).astype(BF16)
    bands = jnp.dot(picked, same_view, preferred_element_type=F32)

    slot = col >> 7
    third = jnp.where(first_half, tile - 1, tile + 1)
    pair = jnp.where(first_half, tile + 1, tile - 1)
    source = jnp.where(slot == 0, tile, jnp.where(slot == 1, pair, third))
    col_row = jnp.where((source >= 0) & (source < 32), source * TILE + (col & 31), -100000)
    reach = (col_row - row).astype(F32) - bands

    rest = lane - 4 * VIEWS
    lane_slice = jnp.where(rest < 0, lane & 3, (rest >> 2) & 3)
    rest_c = lane_c - 4 * VIEWS
    lane_view = jnp.where(rest_c < 0, lane_c >> 2, rest_c >> 4)
    last_slice = 32 * HERE - 1
    kinds = [rest < 0] + [(rest >= 0) & (rest < 64) & ((rest & 3) == k) for k in range(BAND)]
    held = []
    for i in range(DEEP):
        at = depth * HERE + (i - 2)
        at = jnp.where(at < 0, -1 - at, jnp.where(at > last_slice, 2 * last_slice + 1 - at, at))
        mine = prm_ref[pl.ds((at >> 2) - depth + 1, 1), :]
        held.append(jnp.where(lane_slice == (at & 3), mine, 0.0))
    held = jnp.concatenate(held, axis=0)
    stacked = jnp.concatenate([jnp.where(kind, held, 0.0) for kind in kinds], axis=0)
    spread = ((lane_view == view_c) & (rest_c < 64)).astype(F32).astype(BF16)
    table = jnp.dot(stacked.astype(BF16), spread, preferred_element_type=F32)

    parts = []
    for i in range(DEEP):
        gap = reach - table[i : i + 1, :]
        weight = jnp.zeros((ROWS, SPAN), F32)
        for k in range(BAND):
            at = (k + 1) * DEEP + i
            weight = jnp.where(gap == float(k), table[at : at + 1, :], weight)
        parts.append(weight)
    return jnp.concatenate(parts, axis=0).astype(BF16)


def sweep(src, flow, count, rows, tiles, store):
    lane = lax.broadcasted_iota(I32, (rows, LANES), 1)
    first, last = lane == 0, lane == LANES - 1

    def at(t):
        return slice(t * LANES, (t + 1) * LANES)

    for t in range(tiles):
        flow[:rows, at(t)] = half_conduct(src[1, :rows, at(t)] - src[0, :rows, at(t)])

    def one(i, carry):
        came = 0.0
        for t0 in range(0, tiles, BATCH):
            batch = range(t0, min(t0 + BATCH, tiles))
            tall = [src[i + 1, :, at(t)] for t in batch]
            ahead = [src[i + 2, :rows, at(t)] for t in batch]
            behind = [flow[:rows, at(t)] for t in batch]
            centre = [x[:rows] for x in tall]
            turned = [pltpu.roll(x, LANES - 1, 1) for x in centre]
            if t0 + BATCH < tiles:
                turned.append(pltpu.roll(src[i + 1, :rows, at(t0 + BATCH)], LANES - 1, 1))
            ahead = [half_conduct(x - c) for x, c in zip(ahead, centre)]
            total = [x - y for x, y in zip(ahead, behind)]
            step = [half_conduct(pltpu.roll(x, ROWS - 1, 0) - x) for x in tall]
            step = [(x - pltpu.roll(x, 1, 0))[:rows] for x in step]
            total = [x + y for x, y in zip(total, step)]
            step = []
            for n in range(len(batch)):
                if n + 1 < len(turned):
                    right = jnp.where(last, turned[n + 1], turned[n])
                    step.append(half_conduct(right - centre[n]))
                else:
                    step.append(jnp.where(last, 0.0, half_conduct(turned[n] - centre[n])))
            goes = [pltpu.roll(x, 1, 1) for x in step]
            total = [x + y for x, y in zip(total, step)]
            left = [jnp.where(first, x, y) for x, y in zip([came] + goes, goes)]
            came = goes[-1]
            total = [c + RATE4 * (x - y) for c, x, y in zip(centre, total, left)]
            for n, t in enumerate(batch):
                flow[:rows, at(t)] = ahead[n]
            for n, t in enumerate(batch):
                store(i, at(t), total[n])
        return carry

    lax.fori_loop(0, count, one, 0)


def half(second, ids, prm_ref, band_ref, own_ref, *rest):
    if second:
        other_ref, _, out_ref, weights, v0, v1, flow, done, sems = rest
    else:
        out_ref, weights, v0, v1, flow, done, sems = rest
    xh, core, xl = ids[2], ids[3], ids[4]
    tiles = TILES + 2 if second else TILES

    def band(ref):
        return ref[8 * SIZE :, :].astype(F32)[:1, :]

    pair_band = band(own_ref.at[2 * (1 - xh)])
    weights[...] = interpolation(ids, prm_ref, band_ref[...], pair_band, band(own_ref.at[4]))

    def project(pieces, x, y, count, first):
        columns = []
        for i in range(count):
            at = pl.ds(pl.multiple_of((y + i) * SIZE, SIZE), SIZE)
            near = pieces[2 * xh + x, at, :]
            pair = pieces[2 * (1 - xh) + x, at, :]
            third = pieces[4 + (x ^ xl), at, :]
            columns.append(jnp.concatenate([near, pair, third], axis=0))
        found = jnp.dot(
            weights[...], jnp.concatenate(columns, axis=1), preferred_element_type=F32
        )
        where = pl.ds(pl.multiple_of(first * LANES, LANES), count * LANES)
        v0[:, :, where] = found.reshape(DEEP, ROWS, count * LANES)

    if second:
        before = (1 - core) * 2
        project(other_ref, 0, 0, 8, before)
        project(other_ref, 1, 0, 8, before + 8)
        project(own_ref, 1 - core, 6 * (1 - core), 2, core * TILES)
    else:
        project(own_ref, 0, 0, 8, 0)
        project(own_ref, 1, 0, 8, 8)

    def keep(i, at, value):
        v1[i, :, at] = value

    sweep(v0, flow, HERE + 2, ROWS, tiles, keep)

    count = (tiles - 1 if second else tiles) * LANES
    source, target = 0, pl.multiple_of(core * (NC // 2), LANES)
    if second:
        source = pl.multiple_of((1 - core) * LANES, LANES)
        target = pl.multiple_of((1 - core) * (TILES - 1) * LANES, LANES)

    def copy(i):
        return pltpu.make_async_copy(
            done.at[i, :, pl.ds(source, count)],
            out_ref.at[i, :, pl.ds(target, count)],
            sems.at[i],
        )

    def put(i, at, value):
        done[i, :, at] = value
        if at.stop == tiles * LANES:
            copy(i).start()

    sweep(v1, flow, HERE, TILE, tiles, put)
    for i in range(HERE):
        copy(i).wait()


def smooth(second, *operands):
    wide = (TILES + 2 if second else TILES) * LANES
    whole = pl.BlockSpec(memory_space=pltpu.VMEM)
    specs = [pl.BlockSpec(memory_space=pltpu.SMEM)] + [whole] * (4 if second else 3)
    if second:
        specs.append(pl.BlockSpec(memory_space=pl.ANY))
    return pl.pallas_call(
        functools.partial(half, second),
        out_shape=jax.ShapeDtypeStruct((HERE, TILE, NC), F32),
        in_specs=specs,
        out_specs=pl.BlockSpec(memory_space=pl.ANY),
        scratch_shapes=[
            pltpu.VMEM((DEEP * ROWS, SPAN), BF16),
            pltpu.VMEM((DEEP, ROWS, wide), F32),
            pltpu.VMEM((HERE + 2, ROWS, wide), F32),
            pltpu.VMEM((ROWS, wide), F32),
            pltpu.VMEM((HERE, TILE, wide), F32),
            pltpu.SemaphoreType.DMA((HERE,)),
        ],
        input_output_aliases={5: 0} if second else {},
        cost_estimate=pl.CostEstimate(
            flops=2 * DEEP * ROWS * SPAN * wide,
            bytes_accessed=24 * 1024 * 1024,
            transcendentals=0,
        ),
        compiler_params=pltpu.CompilerParams(vmem_limit_bytes=24 * 1024 * 1024),
    )(*operands)


def pack(stored_ref, offset_ref, taps_ref, out_ref, numbers_ref):
    lane = lax.broadcasted_iota(I32, (1, LANES), 1)
    rest = lane - 4 * VIEWS
    line = lax.broadcasted_iota(I32, (HERE, LANES), 0)
    pick = (line == (lane & 3)).astype(F32)
    spread = jnp.dot(offset_ref[...].astype(F32), pick, preferred_element_type=F32)
    mine = (line == (lane >> 2)) & (lane < 4 * VIEWS)
    numbers = jnp.sum(jnp.where(mine, spread, 0.0), axis=0, keepdims=True)
    for v in range(VIEWS):
        spread = jnp.dot(taps_ref[v].astype(F32), pick, preferred_element_type=F32)
        mine = (line == ((rest >> 2) & 3)) & (rest >= 0) & ((rest >> 4) == v)
        numbers += jnp.sum(jnp.where(mine, spread, 0.0), axis=0, keepdims=True)
    numbers_ref[...] = jnp.broadcast_to(numbers, (16, LANES)).astype(BF16)
    for y in range(8):
        for xl in range(2):
            for core in range(2):
                at = ((core * 2 + xl) * 8 + y) * LANES
                out_ref[(y * 2 + xl) * 2 + core] = stored_ref[:, at : at + LANES]


def shards(projections, owner, row_offset, band_start, taps):
    xh, xl, core = (lax.axis_index(a) for a in ("xh", "xl", "core"))
    depth, tile = lax.axis_index(DEPTH), lax.axis_index(("z", "xh"))
    ids = jnp.stack([depth, tile, xh, core, xl]).astype(I32)

    whole = pl.BlockSpec(memory_space=pltpu.VMEM)
    pieces, numbers = pl.pallas_call(
        pack,
        out_shape=(
            jax.ShapeDtypeStruct((32, TILE, LANES), BF16),
            jax.ShapeDtypeStruct((16, LANES), BF16),
        ),
        in_specs=[whole] * 3,
        out_specs=[whole] * 2,
    )(projections[0], row_offset, taps)
    got = lax.all_to_all(pieces, DEPTH, 0, 0, tiled=True)
    views = jnp.concatenate(
        [lax.dynamic_index_in_dim(got, owner[v], keepdims=False) for v in range(VIEWS)]
    )

    band = band_start.astype(BF16).reshape(1, SIZE)
    rest = (band.astype(F32), jnp.pad(band, ((0, 15), (0, 0))), ids, numbers)
    views, (band, band_rows, ids, numbers) = lax.optimization_barrier((views, rest))
    near = lax.all_to_all(jnp.broadcast_to(views[None], (8, SIZE, LANES)), "y", 0, 0, tiled=True)
    near = jnp.concatenate([near.reshape(8 * SIZE, LANES), band_rows])

    shift = [(2 * i + 2, 2 * i) for i in range(15)] + [(2 * i + 1, 2 * i + 3) for i in range(15)]
    foreign = lax.ppermute(near, ("z", "xh"), shift)
    own = lax.all_to_all(
        jnp.broadcast_to(near[None], (4,) + near.shape), ("xh", "xl"), 0, 0, tiled=True
    )

    lower = lax.ppermute(numbers, DEPTH, [(i, i + 1) for i in range(31)])
    upper = lax.ppermute(numbers, DEPTH, [(i + 1, i) for i in range(31)])
    own, foreign, lower, upper = lax.optimization_barrier((own, foreign, lower, upper))
    prm = jnp.concatenate([lower[:1], numbers[:1], upper[:1]]).astype(F32)

    along = [(a, b) for b, a in shift]
    third = lax.dynamic_slice(
        own, (2 * (1 - xh) + xl, 0, 0), (1,) + near.shape, allow_negative_indices=False
    )[0]
    third = lax.ppermute(third, ("z", "xh"), along)
    third_far = lax.ppermute(foreign, ("xl", "xh"), [(0, 3), (1, 2), (2, 1), (3, 0)])

    swap = [(0, 1), (1, 0)]
    own = jnp.concatenate([own, third[None], third_far[None]])
    other = lax.ppermute(own, "core", swap)
    first = smooth(False, ids, prm, band, own)
    return smooth(True, ids, prm, band, own, other, first)


def solution(mesh):
    parted = Mesh(mesh.devices.reshape(8, 2, 2, 16, 2), DEPTH + ("z", "xh"))
    rows = ("z", "xh")
    placed = (
        P(DEPTH, rows, None),
        P(),
        P(None, DEPTH),
        P(None, rows),
        P(None, DEPTH, None),
    )
    return jax.shard_map(
        shards, mesh=parted, in_specs=placed, out_specs=P(DEPTH, rows, None), check_vma=False
    )
```

```python
import functools

import jax
import jax.numpy as jnp
from jax import lax
from jax.experimental import pallas as pl
from jax.experimental.pallas import tpu as pltpu
from jax.sharding import Mesh, PartitionSpec as P

RATE4 = 0.56
F32 = jnp.float32
BF16 = jnp.bfloat16
I32 = jnp.int32

TILE = 32
HERE = 4
VIEWS = 4
BAND = 4
LANES = 128
NC = 4096
SIZE = VIEWS * TILE
TILES = NC // LANES // 2
SPAN = 3 * VIEWS * TILE
ROWS = 40
DEEP = HERE + 4
BATCH = 16
DEPTH = ("y", "xl", "core")


def half_conduct(diff):
    return diff / (diff * diff + 4.0)


def interpolation(ids, prm_ref, here, pair, away):
    depth, tile, xh = ids[0], ids[1], ids[2]
    lane = lax.broadcasted_iota(I32, (1, LANES), 1)
    col = lax.broadcasted_iota(I32, (1, SPAN), 1)
    view_of_col = (col >> 5) & 3
    lane_c = lax.broadcasted_iota(I32, (LANES, SPAN), 0)
    view_c = (lax.broadcasted_iota(I32, (LANES, SPAN), 1) >> 5) & 3

    row = lax.broadcasted_iota(I32, (ROWS, 1), 0)
    row = tile * TILE + jnp.where(row < 36, row, row - ROWS)
    last = 32 * TILE - 1
    row = jnp.where(row < 0, -1 - row, jnp.where(row > last, 2 * last + 1 - row, row))
    row_tile = row >> 5
    first_half = xh == 0
    before = jnp.where(first_half, away, pair)
    after = jnp.where(first_half, pair, away)
    picked = jnp.where(row_tile == tile, here, jnp.where(row_tile < tile, before, after))
    picked = jnp.where((lane & 31) == (row & 31), picked, 0.0).astype(BF16)
    same_view = ((lane_c >> 5) == view_c).astype(F32).astype(BF16)
    bands = jnp.dot(picked, same_view, preferred_element_type=F32)

    slot = col >> 7
    third = jnp.where(first_half, tile - 1, tile + 1)
    pair = jnp.where(first_half, tile + 1, tile - 1)
    source = jnp.where(slot == 0, tile, jnp.where(slot == 1, pair, third))
    col_row = jnp.where((source >= 0) & (source < 32), source * TILE + (col & 31), -100000)
    reach = (col_row - row).astype(F32) - bands

    rest = lane - 4 * VIEWS
    lane_slice = jnp.where(rest < 0, lane & 3, (rest >> 2) & 3)
    rest_c = lane_c - 4 * VIEWS
    lane_view = jnp.where(rest_c < 0, lane_c >> 2, rest_c >> 4)
    last_slice = 32 * HERE - 1
    kinds = [rest < 0] + [(rest >= 0) & (rest < 64) & ((rest & 3) == k) for k in range(BAND)]
    held = []
    for i in range(DEEP):
        at = depth * HERE + (i - 2)
        at = jnp.where(at < 0, -1 - at, jnp.where(at > last_slice, 2 * last_slice + 1 - at, at))
        mine = prm_ref[pl.ds(at >> 2, 1), :]
        held.append(jnp.where(lane_slice == (at & 3), mine, 0.0))
    held = jnp.concatenate(held, axis=0)
    stacked = jnp.concatenate([jnp.where(kind, held, 0.0) for kind in kinds], axis=0)
    spread = ((lane_view == view_c) & (rest_c < 64)).astype(F32).astype(BF16)
    table = jnp.dot(stacked.astype(BF16), spread, preferred_element_type=F32)

    parts = []
    for i in range(DEEP):
        gap = reach - table[i : i + 1, :]
        weight = jnp.zeros((ROWS, SPAN), F32)
        for k in range(BAND):
            at = (k + 1) * DEEP + i
            weight = jnp.where(gap == float(k), table[at : at + 1, :], weight)
        parts.append(weight)
    return jnp.concatenate(parts, axis=0).astype(BF16)


def sweep(src, flow, count, rows, tiles, store):
    lane = lax.broadcasted_iota(I32, (rows, LANES), 1)
    first, last = lane == 0, lane == LANES - 1

    def at(t):
        return slice(t * LANES, (t + 1) * LANES)

    for t in range(tiles):
        flow[:rows, at(t)] = half_conduct(src[1, :rows, at(t)] - src[0, :rows, at(t)])

    def one(i, carry):
        came = 0.0
        for t0 in range(0, tiles, BATCH):
            batch = range(t0, min(t0 + BATCH, tiles))
            tall = [src[i + 1, :, at(t)] for t in batch]
            ahead = [src[i + 2, :rows, at(t)] for t in batch]
            behind = [flow[:rows, at(t)] for t in batch]
            centre = [x[:rows] for x in tall]
            turned = [pltpu.roll(x, LANES - 1, 1) for x in centre]
            if t0 + BATCH < tiles:
                turned.append(pltpu.roll(src[i + 1, :rows, at(t0 + BATCH)], LANES - 1, 1))
            ahead = [half_conduct(x - c) for x, c in zip(ahead, centre)]
            total = [x - y for x, y in zip(ahead, behind)]
            step = [half_conduct(pltpu.roll(x, ROWS - 1, 0) - x) for x in tall]
            step = [(x - pltpu.roll(x, 1, 0))[:rows] for x in step]
            total = [x + y for x, y in zip(total, step)]
            step = []
            for n in range(len(batch)):
                if n + 1 < len(turned):
                    right = jnp.where(last, turned[n + 1], turned[n])
                    step.append(half_conduct(right - centre[n]))
                else:
                    step.append(jnp.where(last, 0.0, half_conduct(turned[n] - centre[n])))
            goes = [pltpu.roll(x, 1, 1) for x in step]
            total = [x + y for x, y in zip(total, step)]
            left = [jnp.where(first, x, y) for x, y in zip([came] + goes, goes)]
            came = goes[-1]
            total = [c + RATE4 * (x - y) for c, x, y in zip(centre, total, left)]
            for n, t in enumerate(batch):
                flow[:rows, at(t)] = ahead[n]
            for n, t in enumerate(batch):
                store(i, at(t), total[n])
        return carry

    lax.fori_loop(0, count, one, 0)


def half(second, ids, prm_ref, band_ref, own_ref, *rest):
    if second:
        other_ref, _, out_ref, weights, v0, v1, flow, done, sems = rest
    else:
        out_ref, weights, v0, v1, flow, done, sems = rest
    core, xl = ids[3], ids[4]
    tiles = TILES + 2 if second else TILES

    def band(ref):
        return ref[8 * SIZE :, :].astype(F32)[:1, :]

    pair_band = band(own_ref.at[3])
    weights[...] = interpolation(ids, prm_ref, band_ref[...], pair_band, band(own_ref.at[5]))

    def project(pieces, x, y, count, first):
        columns = []
        for i in range(count):
            at = pl.ds(pl.multiple_of((y + i) * SIZE, SIZE), SIZE)
            from_tiles = [pieces[2 * n + (x ^ xl), at, :] for n in range(3)]
            columns.append(jnp.concatenate(from_tiles, axis=0))
        found = jnp.dot(
            weights[...], jnp.concatenate(columns, axis=1), preferred_element_type=F32
        )
        where = pl.ds(pl.multiple_of(first * LANES, LANES), count * LANES)
        v0[:, :, where] = found.reshape(DEEP, ROWS, count * LANES)

    if second:
        before = (1 - core) * 2
        project(other_ref, 0, 0, 8, before)
        project(other_ref, 1, 0, 8, before + 8)
        project(own_ref, 1 - core, 6 * (1 - core), 2, core * TILES)
    else:
        project(own_ref, 0, 0, 8, 0)
        project(own_ref, 1, 0, 8, 8)

    def keep(i, at, value):
        v1[i, :, at] = value

    sweep(v0, flow, HERE + 2, ROWS, tiles, keep)

    count = (tiles - 1 if second else tiles) * LANES
    source, target = 0, pl.multiple_of(core * (NC // 2), LANES)
    if second:
        source = pl.multiple_of((1 - core) * LANES, LANES)
        target = pl.multiple_of((1 - core) * (TILES - 1) * LANES, LANES)

    def copy(i):
        return pltpu.make_async_copy(
            done.at[i, :, pl.ds(source, count)],
            out_ref.at[i, :, pl.ds(target, count)],
            sems.at[i],
        )

    def put(i, at, value):
        done[i, :, at] = value
        if at.stop == tiles * LANES:
            copy(i).start()

    sweep(v1, flow, HERE, TILE, tiles, put)
    for i in range(HERE):
        copy(i).wait()


def smooth(second, *operands):
    wide = (TILES + 2 if second else TILES) * LANES
    whole = pl.BlockSpec(memory_space=pltpu.VMEM)
    specs = [pl.BlockSpec(memory_space=pltpu.SMEM)] + [whole] * (4 if second else 3)
    if second:
        specs.append(pl.BlockSpec(memory_space=pl.ANY))
    return pl.pallas_call(
        functools.partial(half, second),
        out_shape=jax.ShapeDtypeStruct((HERE, TILE, NC), F32),
        in_specs=specs,
        out_specs=pl.BlockSpec(memory_space=pl.ANY),
        scratch_shapes=[
            pltpu.VMEM((DEEP * ROWS, SPAN), BF16),
            pltpu.VMEM((DEEP, ROWS, wide), F32),
            pltpu.VMEM((HERE + 2, ROWS, wide), F32),
            pltpu.VMEM((ROWS, wide), F32),
            pltpu.VMEM((HERE, TILE, wide), F32),
            pltpu.SemaphoreType.DMA((HERE,)),
        ],
        input_output_aliases={5: 0} if second else {},
        cost_estimate=pl.CostEstimate(
            flops=2 * DEEP * ROWS * SPAN * wide,
            bytes_accessed=24 * 1024 * 1024,
            transcendentals=0,
        ),
        compiler_params=pltpu.CompilerParams(vmem_limit_bytes=24 * 1024 * 1024),
    )(*operands)


def pack(stored_ref, offset_ref, taps_ref, out_ref):
    lane = lax.broadcasted_iota(I32, (1, LANES), 1)
    rest = lane - 4 * VIEWS
    line = lax.broadcasted_iota(I32, (HERE, LANES), 0)
    pick = (line == (lane & 3)).astype(F32)
    spread = jnp.dot(offset_ref[...].astype(F32), pick, preferred_element_type=F32)
    mine = (line == (lane >> 2)) & (lane < 4 * VIEWS)
    numbers = jnp.sum(jnp.where(mine, spread, 0.0), axis=0, keepdims=True)
    for v in range(VIEWS):
        spread = jnp.dot(taps_ref[v].astype(F32), pick, preferred_element_type=F32)
        mine = (line == ((rest >> 2) & 3)) & (rest >= 0) & ((rest >> 4) == v)
        numbers += jnp.sum(jnp.where(mine, spread, 0.0), axis=0, keepdims=True)
    numbers = jnp.broadcast_to(numbers, (8, LANES)).astype(BF16)
    for y in range(8):
        for xl in range(2):
            for core in range(2):
                at = ((core * 2 + xl) * 8 + y) * LANES
                piece = stored_ref[:, at : at + LANES]
                out_ref[(y * 2 + xl) * 2 + core] = jnp.concatenate([piece, numbers], axis=0)


def shards(projections, owner, row_offset, band_start, taps):
    xh, xl, core = (lax.axis_index(a) for a in ("xh", "xl", "core"))
    depth, tile = lax.axis_index(DEPTH), lax.axis_index(("z", "xh"))
    ids = jnp.stack([depth, tile, xh, core, xl]).astype(I32)

    whole = pl.BlockSpec(memory_space=pltpu.VMEM)
    pieces = pl.pallas_call(
        pack,
        out_shape=jax.ShapeDtypeStruct((32, TILE + 8, LANES), BF16),
        in_specs=[whole] * 3,
        out_specs=whole,
    )(projections[0], row_offset, taps)
    got = lax.all_to_all(pieces, DEPTH, 0, 0, tiled=True)
    prm = got[:, TILE, :].astype(F32)
    views = jnp.concatenate(
        [lax.dynamic_index_in_dim(got, owner[v], keepdims=False)[:TILE] for v in range(VIEWS)]
    )

    band = band_start.astype(BF16).reshape(1, SIZE)
    rest = (band.astype(F32), jnp.pad(band, ((0, 15), (0, 0))), prm, ids)
    views, (band, band_rows, prm, ids) = lax.optimization_barrier((views, rest))
    near = lax.all_to_all(jnp.broadcast_to(views[None], (8, SIZE, LANES)), "y", 0, 0, tiled=True)
    near = jnp.concatenate([near.reshape(8 * SIZE, LANES), band_rows])

    swap = [(0, 1), (1, 0)]
    across = [(0, 3), (1, 2), (2, 1), (3, 0)]
    pair_far = lax.ppermute(near, ("xl", "xh"), across)
    on = [((x * 16 + i + 1) * 2, ((1 - x) * 16 + i) * 2) for i in range(15) for x in range(2)]
    on += [(a + 1 - 2, b + 1 + 2) for a, b in on]
    foreign = lax.ppermute(near, ("xl", "z", "xh"), on)
    near_far = lax.ppermute(near, "xl", swap)

    along = [(2 * i, 2 * i + 2) for i in range(15)] + [(2 * i + 3, 2 * i + 1) for i in range(15)]
    third_far = lax.ppermute(pair_far, ("z", "xh"), along)
    third = lax.ppermute(foreign, ("xl", "xh"), across)
    upper = lax.ppermute(near_far[: 4 * SIZE], ("xl", "xh"), across)
    lower = lax.ppermute(pair_far[4 * SIZE :], "xl", swap)

    pair = jnp.concatenate([upper, lower])
    own = jnp.stack([near, near_far, pair, pair_far, third, third_far])
    other = lax.ppermute(own, "core", swap)
    first = smooth(False, ids, prm, band, own)
    return smooth(True, ids, prm, band, own, other, first)


def solution(mesh):
    parted = Mesh(mesh.devices.reshape(8, 2, 2, 16, 2), DEPTH + ("z", "xh"))
    rows = ("z", "xh")
    placed = (
        P(DEPTH, rows, None),
        P(),
        P(None, DEPTH),
        P(None, rows),
        P(None, DEPTH, None),
    )
    return jax.shard_map(
        shards, mesh=parted, in_specs=placed, out_specs=P(DEPTH, rows, None), check_vma=False
    )
```

```python
import functools

import jax
import jax.numpy as jnp
from jax import lax
from jax.experimental import pallas as pl
from jax.experimental.pallas import tpu as pltpu
from jax.sharding import Mesh, PartitionSpec as P

RATE4 = 0.56
F32 = jnp.float32
BF16 = jnp.bfloat16
I32 = jnp.int32

TILE = 32
HERE = 4
VIEWS = 4
BAND = 4
LANES = 128
NC = 4096
SIZE = VIEWS * TILE
TILES = NC // LANES // 2
SPAN = 3 * VIEWS * TILE
ROWS = 40
DEEP = HERE + 4
BATCH = 16
ALONG_Y = ("ya", "yb")
DEPTH = ALONG_Y + ("xl", "core")


def half_conduct(diff):
    return diff / (diff * diff + 4.0)


def interpolation(ids, prm_ref, here, pair, away):
    depth, tile, xh = ids[0], ids[1], ids[2]
    lane = lax.broadcasted_iota(I32, (1, LANES), 1)
    col = lax.broadcasted_iota(I32, (1, SPAN), 1)
    row_of_col = ((col >> 5) & 3) * 8 + (col & 7)
    lane_c = lax.broadcasted_iota(I32, (LANES, SPAN), 0)
    view_c = (lax.broadcasted_iota(I32, (LANES, SPAN), 1) >> 3) & 3

    row = lax.broadcasted_iota(I32, (ROWS, 1), 0)
    row = tile * TILE + jnp.where(row < 36, row, row - ROWS)
    last = 32 * TILE - 1
    row = jnp.where(row < 0, -1 - row, jnp.where(row > last, 2 * last + 1 - row, row))
    row_tile = row >> 5
    first_half = xh == 0
    before = jnp.where(first_half, away, pair)
    after = jnp.where(first_half, pair, away)
    picked = jnp.where(row_tile == tile, here, jnp.where(row_tile < tile, before, after))
    picked = jnp.where((lane & 31) == (row & 31), picked, 0.0).astype(BF16)
    same_view = ((lane_c >> 5) == view_c).astype(F32).astype(BF16)
    bands = jnp.dot(picked, same_view, preferred_element_type=F32)

    slot = col >> 7
    third = jnp.where(first_half, tile - 1, tile + 1)
    pair = jnp.where(first_half, tile + 1, tile - 1)
    source = jnp.where(slot == 0, tile, jnp.where(slot == 1, pair, third))
    col_row = jnp.where((source >= 0) & (source < 32), source * TILE + row_of_col, -100000)
    reach = (col_row - row).astype(F32) - bands

    rest = lane - 4 * VIEWS
    lane_slice = jnp.where(rest < 0, lane & 3, (rest >> 2) & 3)
    rest_c = lane_c - 4 * VIEWS
    lane_view = jnp.where(rest_c < 0, lane_c >> 2, rest_c >> 4)
    last_slice = 32 * HERE - 1
    kinds = [rest < 0] + [(rest >= 0) & (rest < 64) & ((rest & 3) == k) for k in range(BAND)]
    held = []
    for i in range(DEEP):
        at = depth * HERE + (i - 2)
        at = jnp.where(at < 0, -1 - at, jnp.where(at > last_slice, 2 * last_slice + 1 - at, at))
        mine = prm_ref[pl.ds((at >> 2) - depth + 1, 1), :]
        held.append(jnp.where(lane_slice == (at & 3), mine, 0.0))
    held = jnp.concatenate(held, axis=0)
    stacked = jnp.concatenate([jnp.where(kind, held, 0.0) for kind in kinds], axis=0)
    spread = ((lane_view == view_c) & (rest_c < 64)).astype(F32).astype(BF16)
    table = jnp.dot(stacked.astype(BF16), spread, preferred_element_type=F32)

    parts = []
    for i in range(DEEP):
        gap = reach - table[i : i + 1, :]
        weight = jnp.zeros((ROWS, SPAN), F32)
        for k in range(BAND):
            at = (k + 1) * DEEP + i
            weight = jnp.where(gap == float(k), table[at : at + 1, :], weight)
        parts.append(weight)
    return jnp.concatenate(parts, axis=0).astype(BF16)


def sweep(src, flow, count, rows, tiles, store):
    lane = lax.broadcasted_iota(I32, (rows, LANES), 1)
    first, last = lane == 0, lane == LANES - 1

    def at(t):
        return slice(t * LANES, (t + 1) * LANES)

    for t in range(tiles):
        flow[:rows, at(t)] = half_conduct(src[1, :rows, at(t)] - src[0, :rows, at(t)])

    def one(i, carry):
        came = 0.0
        for t0 in range(0, tiles, BATCH):
            batch = range(t0, min(t0 + BATCH, tiles))
            tall = [src[i + 1, :, at(t)] for t in batch]
            ahead = [src[i + 2, :rows, at(t)] for t in batch]
            behind = [flow[:rows, at(t)] for t in batch]
            centre = [x[:rows] for x in tall]
            turned = [pltpu.roll(x, LANES - 1, 1) for x in centre]
            if t0 + BATCH < tiles:
                turned.append(pltpu.roll(src[i + 1, :rows, at(t0 + BATCH)], LANES - 1, 1))
            ahead = [half_conduct(x - c) for x, c in zip(ahead, centre)]
            total = [x - y for x, y in zip(ahead, behind)]
            step = [half_conduct(pltpu.roll(x, ROWS - 1, 0) - x) for x in tall]
            step = [(x - pltpu.roll(x, 1, 0))[:rows] for x in step]
            total = [x + y for x, y in zip(total, step)]
            step = []
            for n in range(len(batch)):
                if n + 1 < len(turned):
                    right = jnp.where(last, turned[n + 1], turned[n])
                    step.append(half_conduct(right - centre[n]))
                else:
                    step.append(jnp.where(last, 0.0, half_conduct(turned[n] - centre[n])))
            goes = [pltpu.roll(x, 1, 1) for x in step]
            total = [x + y for x, y in zip(total, step)]
            left = [jnp.where(first, x, y) for x, y in zip([came] + goes, goes)]
            came = goes[-1]
            total = [c + RATE4 * (x - y) for c, x, y in zip(centre, total, left)]
            for n, t in enumerate(batch):
                flow[:rows, at(t)] = ahead[n]
            for n, t in enumerate(batch):
                store(i, at(t), total[n])
        return carry

    lax.fori_loop(0, count, one, 0)


def half(second, ids, prm_ref, band_ref, own_ref, *rest):
    if second:
        other_ref, _, out_ref, weights, v0, v1, flow, done, sems = rest
    else:
        out_ref, weights, v0, v1, flow, done, sems = rest
    xh, core, xl = ids[2], ids[3], ids[4]
    tiles = TILES + 2 if second else TILES

    def band(ref):
        return ref[8 * SIZE :, :].astype(F32)[:1, :]

    pair_band = band(own_ref.at[2 * (1 - xh)])
    weights[...] = interpolation(ids, prm_ref, band_ref[...], pair_band, band(own_ref.at[4]))

    def project(pieces, start, count, first):
        columns = []
        for i in range(count):
            tile = start + i
            yb, x = tile >> 3, (tile >> 2) & 1
            parts = []
            for part in (2 * xh + x, 2 * (1 - xh) + x, 4 + (x ^ xl)):
                for ya in range(4):
                    at = pl.multiple_of((2 * ya + yb) * SIZE + (tile & 3) * TILE, TILE)
                    parts.append(pieces[part, pl.ds(at, TILE), :])
            columns.append(jnp.concatenate(parts, axis=0))
        found = jnp.dot(
            weights[...], jnp.concatenate(columns, axis=1), preferred_element_type=F32
        )
        where = pl.ds(pl.multiple_of(first * LANES, LANES), count * LANES)
        v0[:, :, where] = found.reshape(DEEP, ROWS, count * LANES)

    if second:
        before = (1 - core) * 2
        project(other_ref, 0, 8, before)
        project(other_ref, 8, 8, before + 8)
        project(own_ref, 14 * (1 - core), 2, core * TILES)
    else:
        project(own_ref, 0, 8, 0)
        project(own_ref, 8, 8, 8)

    def keep(i, at, value):
        v1[i, :, at] = value

    sweep(v0, flow, HERE + 2, ROWS, tiles, keep)

    count = (tiles - 1 if second else tiles) * LANES
    source, target = 0, pl.multiple_of(core * (NC // 2), LANES)
    if second:
        source = pl.multiple_of((1 - core) * LANES, LANES)
        target = pl.multiple_of((1 - core) * (TILES - 1) * LANES, LANES)

    def copy(i):
        return pltpu.make_async_copy(
            done.at[i, :, pl.ds(source, count)],
            out_ref.at[i, :, pl.ds(target, count)],
            sems.at[i],
        )

    def put(i, at, value):
        done[i, :, at] = value
        if at.stop == tiles * LANES:
            copy(i).start()

    sweep(v1, flow, HERE, TILE, tiles, put)
    for i in range(HERE):
        copy(i).wait()


def smooth(second, *operands):
    wide = (TILES + 2 if second else TILES) * LANES
    whole = pl.BlockSpec(memory_space=pltpu.VMEM)
    specs = [pl.BlockSpec(memory_space=pltpu.SMEM)] + [whole] * (4 if second else 3)
    if second:
        specs.append(pl.BlockSpec(memory_space=pl.ANY))
    return pl.pallas_call(
        functools.partial(half, second),
        out_shape=jax.ShapeDtypeStruct((HERE, TILE, NC), F32),
        in_specs=specs,
        out_specs=pl.BlockSpec(memory_space=pl.ANY),
        scratch_shapes=[
            pltpu.VMEM((DEEP * ROWS, SPAN), BF16),
            pltpu.VMEM((DEEP, ROWS, wide), F32),
            pltpu.VMEM((HERE + 2, ROWS, wide), F32),
            pltpu.VMEM((ROWS, wide), F32),
            pltpu.VMEM((HERE, TILE, wide), F32),
            pltpu.SemaphoreType.DMA((HERE,)),
        ],
        input_output_aliases={5: 0} if second else {},
        cost_estimate=pl.CostEstimate(
            flops=2 * DEEP * ROWS * SPAN * wide,
            bytes_accessed=24 * 1024 * 1024,
            transcendentals=0,
        ),
        compiler_params=pltpu.CompilerParams(vmem_limit_bytes=24 * 1024 * 1024),
    )(*operands)


def line_up(offset_ref, taps_ref, numbers_ref):
    lane = lax.broadcasted_iota(I32, (1, LANES), 1)
    rest = lane - 4 * VIEWS
    line = lax.broadcasted_iota(I32, (HERE, LANES), 0)
    pick = (line == (lane & 3)).astype(F32)
    spread = jnp.dot(offset_ref[...].astype(F32), pick, preferred_element_type=F32)
    mine = (line == (lane >> 2)) & (lane < 4 * VIEWS)
    numbers = jnp.sum(jnp.where(mine, spread, 0.0), axis=0, keepdims=True)
    for v in range(VIEWS):
        spread = jnp.dot(taps_ref[v].astype(F32), pick, preferred_element_type=F32)
        mine = (line == ((rest >> 2) & 3)) & (rest >= 0) & ((rest >> 4) == v)
        numbers += jnp.sum(jnp.where(mine, spread, 0.0), axis=0, keepdims=True)
    numbers_ref[...] = jnp.broadcast_to(numbers, (16, LANES)).astype(BF16)


def shards(projections, owner, row_offset, band_start, taps):
    xh, xl, core = (lax.axis_index(a) for a in ("xh", "xl", "core"))
    depth, tile = lax.axis_index(DEPTH), lax.axis_index(("z", "xh"))
    ids = jnp.stack([depth, tile, xh, core, xl]).astype(I32)

    order = ("ya", "core", "yb", "xl")
    pieces = projections[0].reshape(4, 8, 8, 4, LANES).transpose(0, 2, 3, 1, 4)
    got = lax.all_to_all(pieces.reshape(32, TILE, LANES), order, 0, 0, tiled=True)
    place = (owner & 24) + (owner & 1) * 4 + ((owner >> 1) & 3)
    views = jnp.stack(
        [lax.dynamic_index_in_dim(got, place[v], keepdims=False) for v in range(VIEWS)]
    )
    views = views.reshape(VIEWS, 4, 8, LANES).transpose(1, 0, 2, 3).reshape(SIZE, LANES)
    whole = pl.BlockSpec(memory_space=pltpu.VMEM)
    numbers = pl.pallas_call(
        line_up,
        out_shape=jax.ShapeDtypeStruct((16, LANES), BF16),
        in_specs=[whole] * 2,
        out_specs=whole,
    )(row_offset, taps)

    band = band_start.astype(BF16).reshape(1, SIZE)
    rest = (band.astype(F32), jnp.pad(band, ((0, 15), (0, 0))), ids, numbers)
    views, (band, band_rows, ids, numbers) = lax.optimization_barrier((views, rest))
    near = lax.all_to_all(jnp.broadcast_to(views[None], (8, SIZE, LANES)), ALONG_Y, 0, 0, tiled=True)
    near = jnp.concatenate([near.reshape(8 * SIZE, LANES), band_rows])

    shift = [(2 * i + 2, 2 * i) for i in range(15)] + [(2 * i + 1, 2 * i + 3) for i in range(15)]
    foreign = lax.ppermute(near, ("z", "xh"), shift)
    own = lax.all_to_all(
        jnp.broadcast_to(near[None], (4,) + near.shape), ("xh", "xl"), 0, 0, tiled=True
    )

    lower = lax.ppermute(numbers, DEPTH, [(i, i + 1) for i in range(31)])
    upper = lax.ppermute(numbers, DEPTH, [(i + 1, i) for i in range(31)])
    own, foreign, lower, upper = lax.optimization_barrier((own, foreign, lower, upper))
    prm = jnp.concatenate([lower[:1], numbers[:1], upper[:1]]).astype(F32)

    along = [(a, b) for b, a in shift]
    third = lax.dynamic_slice(
        own, (2 * (1 - xh) + xl, 0, 0), (1,) + near.shape, allow_negative_indices=False
    )[0]
    third = lax.ppermute(third, ("z", "xh"), along)
    third_far = lax.ppermute(foreign, ("xl", "xh"), [(0, 3), (1, 2), (2, 1), (3, 0)])

    swap = [(0, 1), (1, 0)]
    own = jnp.concatenate([own, third[None], third_far[None]])
    other = lax.ppermute(own, "core", swap)
    first = smooth(False, ids, prm, band, own)
    return smooth(True, ids, prm, band, own, other, first)


def solution(mesh):
    parted = Mesh(mesh.devices.reshape(4, 2, 2, 2, 16, 2), DEPTH + ("z", "xh"))
    rows = ("z", "xh")
    placed = (
        P(DEPTH, rows, None),
        P(),
        P(None, DEPTH),
        P(None, rows),
        P(None, DEPTH, None),
    )
    return jax.shard_map(
        shards, mesh=parted, in_specs=placed, out_specs=P(DEPTH, rows, None), check_vma=False
    )
```

```python
import functools

import jax
import jax.numpy as jnp
from jax import lax
from jax.experimental import pallas as pl
from jax.experimental.pallas import tpu as pltpu
from jax.sharding import Mesh, PartitionSpec as P

RATE4 = 0.56
F32 = jnp.float32
BF16 = jnp.bfloat16
I32 = jnp.int32

TILE = 32
HERE = 4
VIEWS = 4
BAND = 4
LANES = 128
NC = 4096
SIZE = VIEWS * TILE
TILES = NC // LANES // 2
SPAN = 3 * VIEWS * TILE
ROWS = 40
DEEP = HERE + 4
BATCH = 16
ALONG_Y = ("ya", "yb")
DEPTH = ALONG_Y + ("xl", "core")


def half_conduct(diff):
    return diff / (diff * diff + 4.0)


def interpolation(ids, prm_ref, here, pair, away):
    depth, tile, xh = ids[0], ids[1], ids[2]
    lane = lax.broadcasted_iota(I32, (1, LANES), 1)
    col = lax.broadcasted_iota(I32, (1, SPAN), 1)
    row_of_col = ((col >> 5) & 3) * 8 + (col & 7)
    lane_c = lax.broadcasted_iota(I32, (LANES, SPAN), 0)
    view_c = (lax.broadcasted_iota(I32, (LANES, SPAN), 1) >> 3) & 3

    row = lax.broadcasted_iota(I32, (ROWS, 1), 0)
    row = tile * TILE + jnp.where(row < 36, row, row - ROWS)
    last = 32 * TILE - 1
    row = jnp.where(row < 0, -1 - row, jnp.where(row > last, 2 * last + 1 - row, row))
    row_tile = row >> 5
    first_half = xh == 0
    before = jnp.where(first_half, away, pair)
    after = jnp.where(first_half, pair, away)
    picked = jnp.where(row_tile == tile, here, jnp.where(row_tile < tile, before, after))
    picked = jnp.where((lane & 31) == (row & 31), picked, 0.0).astype(BF16)
    same_view = ((lane_c >> 5) == view_c).astype(F32).astype(BF16)
    bands = jnp.dot(picked, same_view, preferred_element_type=F32)

    slot = col >> 7
    third = jnp.where(first_half, tile - 1, tile + 1)
    pair = jnp.where(first_half, tile + 1, tile - 1)
    source = jnp.where(slot == 0, tile, jnp.where(slot == 1, pair, third))
    col_row = jnp.where((source >= 0) & (source < 32), source * TILE + row_of_col, -100000)
    reach = (col_row - row).astype(F32) - bands

    rest = lane - 4 * VIEWS
    lane_slice = jnp.where(rest < 0, lane & 3, (rest >> 2) & 3)
    rest_c = lane_c - 4 * VIEWS
    lane_view = jnp.where(rest_c < 0, lane_c >> 2, rest_c >> 4)
    last_slice = 32 * HERE - 1
    kinds = [rest < 0] + [(rest >= 0) & (rest < 64) & ((rest & 3) == k) for k in range(BAND)]
    held = []
    for i in range(DEEP):
        at = depth * HERE + (i - 2)
        at = jnp.where(at < 0, -1 - at, jnp.where(at > last_slice, 2 * last_slice + 1 - at, at))
        mine = prm_ref[pl.ds((at >> 2) - depth + 1, 1), :]
        held.append(jnp.where(lane_slice == (at & 3), mine, 0.0))
    held = jnp.concatenate(held, axis=0)
    stacked = jnp.concatenate([jnp.where(kind, held, 0.0) for kind in kinds], axis=0)
    spread = ((lane_view == view_c) & (rest_c < 64)).astype(F32).astype(BF16)
    table = jnp.dot(stacked.astype(BF16), spread, preferred_element_type=F32)

    parts = []
    for i in range(DEEP):
        gap = reach - table[i : i + 1, :]
        weight = jnp.zeros((ROWS, SPAN), F32)
        for k in range(BAND):
            at = (k + 1) * DEEP + i
            weight = jnp.where(gap == float(k), table[at : at + 1, :], weight)
        parts.append(weight)
    return jnp.concatenate(parts, axis=0).astype(BF16)


def sweep(src, flow, count, rows, tiles, store):
    lane = lax.broadcasted_iota(I32, (rows, LANES), 1)
    first, last = lane == 0, lane == LANES - 1

    def at(t):
        return slice(t * LANES, (t + 1) * LANES)

    for t in range(tiles):
        flow[:rows, at(t)] = half_conduct(src[1, :rows, at(t)] - src[0, :rows, at(t)])

    def one(i, carry):
        came = 0.0
        for t0 in range(0, tiles, BATCH):
            batch = range(t0, min(t0 + BATCH, tiles))
            tall = [src[i + 1, :, at(t)] for t in batch]
            ahead = [src[i + 2, :rows, at(t)] for t in batch]
            behind = [flow[:rows, at(t)] for t in batch]
            centre = [x[:rows] for x in tall]
            turned = [pltpu.roll(x, LANES - 1, 1) for x in centre]
            if t0 + BATCH < tiles:
                turned.append(pltpu.roll(src[i + 1, :rows, at(t0 + BATCH)], LANES - 1, 1))
            ahead = [half_conduct(x - c) for x, c in zip(ahead, centre)]
            total = [x - y for x, y in zip(ahead, behind)]
            step = [half_conduct(pltpu.roll(x, ROWS - 1, 0) - x) for x in tall]
            step = [(x - pltpu.roll(x, 1, 0))[:rows] for x in step]
            total = [x + y for x, y in zip(total, step)]
            step = []
            for n in range(len(batch)):
                if n + 1 < len(turned):
                    right = jnp.where(last, turned[n + 1], turned[n])
                    step.append(half_conduct(right - centre[n]))
                else:
                    step.append(jnp.where(last, 0.0, half_conduct(turned[n] - centre[n])))
            goes = [pltpu.roll(x, 1, 1) for x in step]
            total = [x + y for x, y in zip(total, step)]
            left = [jnp.where(first, x, y) for x, y in zip([came] + goes, goes)]
            came = goes[-1]
            total = [c + RATE4 * (x - y) for c, x, y in zip(centre, total, left)]
            for n, t in enumerate(batch):
                flow[:rows, at(t)] = ahead[n]
            for n, t in enumerate(batch):
                store(i, at(t), total[n])
        return carry

    lax.fori_loop(0, count, one, 0)


def half(second, ids, prm_ref, band_ref, own_ref, *rest):
    if second:
        other_ref, _, out_ref, weights, v0, v1, flow, done, sems = rest
    else:
        out_ref, weights, v0, v1, flow, done, sems = rest
    xh, core, xl = ids[2], ids[3], ids[4]
    tiles = TILES + 2 if second else TILES

    def band(ref):
        return ref[8 * SIZE :, :].astype(F32)[:1, :]

    pair_band = band(own_ref.at[2 * (1 - xh)])
    weights[...] = interpolation(ids, prm_ref, band_ref[...], pair_band, band(own_ref.at[4]))

    def project(pieces, start, count, first):
        columns = []
        for i in range(count):
            tile = start + i
            yb, x = tile >> 3, (tile >> 2) & 1
            parts = []
            for part in (2 * xh + x, 2 * (1 - xh) + x, 4 + (x ^ xl)):
                for ya in range(4):
                    at = pl.multiple_of((2 * ya + yb) * SIZE + (tile & 3) * TILE, TILE)
                    parts.append(pieces[part, pl.ds(at, TILE), :])
            columns.append(jnp.concatenate(parts, axis=0))
        found = jnp.dot(
            weights[...], jnp.concatenate(columns, axis=1), preferred_element_type=F32
        )
        where = pl.ds(pl.multiple_of(first * LANES, LANES), count * LANES)
        v0[:, :, where] = found.reshape(DEEP, ROWS, count * LANES)

    if second:
        before = (1 - core) * 2
        project(other_ref, 0, 8, before)
        project(other_ref, 8, 8, before + 8)
        project(own_ref, 14 * (1 - core), 2, core * TILES)
    else:
        project(own_ref, 0, 8, 0)
        project(own_ref, 8, 8, 8)

    def keep(i, at, value):
        v1[i, :, at] = value

    sweep(v0, flow, HERE + 2, ROWS, tiles, keep)

    count = (tiles - 1 if second else tiles) * LANES
    source, target = 0, pl.multiple_of(core * (NC // 2), LANES)
    if second:
        source = pl.multiple_of((1 - core) * LANES, LANES)
        target = pl.multiple_of((1 - core) * (TILES - 1) * LANES, LANES)

    def copy(i):
        return pltpu.make_async_copy(
            done.at[i, :, pl.ds(source, count)],
            out_ref.at[i, :, pl.ds(target, count)],
            sems.at[i],
        )

    def put(i, at, value):
        done[i, :, at] = value
        if at.stop == tiles * LANES:
            copy(i).start()

    sweep(v1, flow, HERE, TILE, tiles, put)
    for i in range(HERE):
        copy(i).wait()


def smooth(second, *operands):
    wide = (TILES + 2 if second else TILES) * LANES
    whole = pl.BlockSpec(memory_space=pltpu.VMEM)
    specs = [pl.BlockSpec(memory_space=pltpu.SMEM)] + [whole] * (4 if second else 3)
    if second:
        specs.append(pl.BlockSpec(memory_space=pl.ANY))
    return pl.pallas_call(
        functools.partial(half, second),
        out_shape=jax.ShapeDtypeStruct((HERE, TILE, NC), F32),
        in_specs=specs,
        out_specs=pl.BlockSpec(memory_space=pl.ANY),
        scratch_shapes=[
            pltpu.VMEM((DEEP * ROWS, SPAN), BF16),
            pltpu.VMEM((DEEP, ROWS, wide), F32),
            pltpu.VMEM((HERE + 2, ROWS, wide), F32),
            pltpu.VMEM((ROWS, wide), F32),
            pltpu.VMEM((HERE, TILE, wide), F32),
            pltpu.SemaphoreType.DMA((HERE,)),
        ],
        input_output_aliases={5: 0} if second else {},
        cost_estimate=pl.CostEstimate(
            flops=2 * DEEP * ROWS * SPAN * wide,
            bytes_accessed=24 * 1024 * 1024,
            transcendentals=0,
        ),
        compiler_params=pltpu.CompilerParams(vmem_limit_bytes=24 * 1024 * 1024),
    )(*operands)


def line_up(offset_ref, taps_ref, numbers_ref):
    lane = lax.broadcasted_iota(I32, (1, LANES), 1)
    rest = lane - 4 * VIEWS
    line = lax.broadcasted_iota(I32, (HERE, LANES), 0)
    pick = (line == (lane & 3)).astype(F32)
    spread = jnp.dot(offset_ref[...].astype(F32), pick, preferred_element_type=F32)
    mine = (line == (lane >> 2)) & (lane < 4 * VIEWS)
    numbers = jnp.sum(jnp.where(mine, spread, 0.0), axis=0, keepdims=True)
    for v in range(VIEWS):
        spread = jnp.dot(taps_ref[v].astype(F32), pick, preferred_element_type=F32)
        mine = (line == ((rest >> 2) & 3)) & (rest >= 0) & ((rest >> 4) == v)
        numbers += jnp.sum(jnp.where(mine, spread, 0.0), axis=0, keepdims=True)
    numbers_ref[...] = jnp.broadcast_to(numbers, (16, LANES)).astype(BF16)


def shards(projections, owner, row_offset, band_start, taps):
    xh, xl, core = (lax.axis_index(a) for a in ("xh", "xl", "core"))
    depth, tile = lax.axis_index(DEPTH), lax.axis_index(("z", "xh"))
    ids = jnp.stack([depth, tile, xh, core, xl]).astype(I32)

    order = ("ya", "core", "yb", "xl")
    pieces = projections[0].reshape(4, 8, 8, 4, LANES).transpose(0, 2, 3, 1, 4)
    got = lax.all_to_all(pieces.reshape(32, TILE, LANES), order, 0, 0, tiled=True)
    place = (owner & 24) + (owner & 1) * 4 + ((owner >> 1) & 3)
    views = jnp.stack(
        [lax.dynamic_index_in_dim(got, place[v], keepdims=False) for v in range(VIEWS)]
    )
    views = views.reshape(VIEWS, 4, 8, LANES).transpose(1, 0, 2, 3).reshape(SIZE, LANES)
    band = band_start.astype(BF16).reshape(1, SIZE)
    rest = (band.astype(F32), jnp.pad(band, ((0, 15), (0, 0))), ids)
    views, (band, band_rows, ids) = lax.optimization_barrier((views, rest))
    near = lax.all_to_all(jnp.broadcast_to(views[None], (8, SIZE, LANES)), ALONG_Y, 0, 0, tiled=True)
    near = jnp.concatenate([near.reshape(8 * SIZE, LANES), band_rows])

    shift = [(2 * i + 2, 2 * i) for i in range(15)] + [(2 * i + 1, 2 * i + 3) for i in range(15)]
    foreign = lax.ppermute(near, ("z", "xh"), shift)
    own = lax.all_to_all(
        jnp.broadcast_to(near[None], (4,) + near.shape), ("xh", "xl"), 0, 0, tiled=True
    )

    _, offsets = lax.optimization_barrier((near, row_offset))
    whole = pl.BlockSpec(memory_space=pltpu.VMEM)
    numbers = pl.pallas_call(
        line_up,
        out_shape=jax.ShapeDtypeStruct((16, LANES), BF16),
        in_specs=[whole] * 2,
        out_specs=whole,
    )(offsets, taps)
    lower = lax.ppermute(numbers, DEPTH, [(i, i + 1) for i in range(31)])
    upper = lax.ppermute(numbers, DEPTH, [(i + 1, i) for i in range(31)])
    own, foreign, lower, upper = lax.optimization_barrier((own, foreign, lower, upper))
    prm = jnp.concatenate([lower[:1], numbers[:1], upper[:1]]).astype(F32)

    along = [(a, b) for b, a in shift]
    third = lax.dynamic_slice(
        own, (2 * (1 - xh) + xl, 0, 0), (1,) + near.shape, allow_negative_indices=False
    )[0]
    third = lax.ppermute(third, ("z", "xh"), along)
    third_far = lax.ppermute(foreign, ("xl", "xh"), [(0, 3), (1, 2), (2, 1), (3, 0)])

    swap = [(0, 1), (1, 0)]
    own = jnp.concatenate([own, third[None], third_far[None]])
    other = lax.ppermute(own, "core", swap)
    first = smooth(False, ids, prm, band, own)
    return smooth(True, ids, prm, band, own, other, first)


def solution(mesh):
    parted = Mesh(mesh.devices.reshape(4, 2, 2, 2, 16, 2), DEPTH + ("z", "xh"))
    rows = ("z", "xh")
    placed = (
        P(DEPTH, rows, None),
        P(),
        P(None, DEPTH),
        P(None, rows),
        P(None, DEPTH, None),
    )
    return jax.shard_map(
        shards, mesh=parted, in_specs=placed, out_specs=P(DEPTH, rows, None), check_vma=False
    )
```
